32 devices in a mesh: pb: 16 (over z, y, x), ga: 2 (over core).
Axes of the slice: x: 2, y: 2, z: 4, core: 2. Of those that a mesh axis runs over, the one named last changes fastest.
Arguments:
- q_of_pair: int32 [4096, 1], P('pb'), may hold values from 0 to 31; in each aligned block of 256 rows (0 to 255, 256 to 511, ...) at most 12 rows name the same one
- q_slot: int32 [32], replicated, may hold values from 0 to 31, each once
- valence: bfloat16 [4096, 16, 1024], P('pb', None, 'ga'), may hold values from -6 to 6
- conduction: bfloat16 [4096, 16, 1024], P('pb', None, 'ga'), may hold values from -0.1875 to 0.1875
- screened: bfloat16 [32, 1024, 1024], P('pb', 'ga'), may hold values from -0.1875 to 0.1875
Outputs:
- kernel_blocks: float32 [4096, 256], P('pb', 'ga')
The draws below stay inside these ranges and needn't reach their ends.
Inputs may be any that keep to these rules, and one draw needn't show every extreme that they name: `q_of_pair`: among the k-pairs of one index of pb (aligned blocks of 256 rows) no q appears more than 12 times, and some q appears exactly 12 times. `q_slot`: each slot is taken by exactly one q.
All inputs are finite; a program needn't handle non-finite values.
Results may differ from the reference program's by a relative error of at most 0.0029.
Values may be sent and summed in bfloat16 or wider, within the bound.
A program may use at most 128 MiB of HBM per device.

```python
import math
import jax
import jax.numpy as jnp
import numpy as np
from jax import lax

NG = 1024
NB = 4
P_DEV = 256
Q_ALL = 32
PAIRS = 4096
CAP = 12


def block_levels(key, shape, pieces, low, largest):
    def one(dim, blocks):
        draws = jax.random.uniform(jax.random.fold_in(jax.random.fold_in(key, 6), dim), (blocks,), jnp.float32, low / len(pieces), largest / len(pieces))
        return jnp.repeat(jnp.exp(draws), shape[dim] // blocks).reshape((-1,) + (1,) * (len(shape) - dim - 1))

    gain = one(*pieces[0])
    for cut in pieces[1:]:
        gain = gain * one(*cut)
    return gain


def assign_block(key, own, number, rows, number_of, top, bound, lean):
    sequence = jax.random.permutation(key, number_of)
    packed, usual = portions_of(number_of, rows * top, bound, lean, True), portions_of(number_of, rows * top, bound, lean, False)
    places = jnp.arange(number_of)

    def named(lengths, rotation):
        used = int((lengths > 0).sum())
        fixed = max(1, used // 4)
        passed = fixed + (places - fixed + rotation * (used - fixed)) % max(1, number_of - fixed)
        return jnp.zeros((number_of,), jnp.int32).at[sequence[jnp.where(places < fixed, places, passed)]].set(jnp.asarray(lengths, jnp.int32))

    lengths = jnp.where(number % 4 == 0, named(packed, number // 4), named(usual, number - number // 4 - 1))
    mixed = jax.random.permutation(jax.random.fold_in(own, 3), number_of)
    donor, receiver = mixed[0:number_of // 2 * 2:2], mixed[1:number_of // 2 * 2:2]
    margin = jnp.minimum(lengths[donor] - 1, bound - lengths[receiver]) // 2
    margin = jnp.where((donor == sequence[0]) | (receiver == sequence[0]) | (lengths[receiver] == 0), 0, jnp.maximum(margin, 0))
    passed = jax.random.randint(jax.random.fold_in(own, 4), (number_of // 2,), 0, 1 << 20) % (margin + 1)
    lengths = lengths.at[donor].add(-passed).at[receiver].add(passed)
    labels = jnp.searchsorted(jnp.cumsum(lengths), jnp.arange(rows * top), side="right").astype(jnp.int32)
    listing = labels.reshape(top, rows).T
    listing = listing[jax.random.permutation(jax.random.fold_in(own, 1), rows)]
    rotation = jax.random.randint(jax.random.fold_in(own, 2), (rows, 1), 0, top)
    return jnp.take_along_axis(listing, (jnp.arange(top)[None, :] + rotation) % top, axis=1)


def portions_of(count, total, bound, lean, full):
    loads = [(1 << 20) // math.isqrt(grade ** lean) + 1 for grade in range(1, count + 1)]
    largest = bound if full else min(bound, max(-(-total // count), total * loads[0] // sum(loads)))
    least = 1 if total - largest >= count - 1 else 0
    given, rest = [largest] + [least] * (count - 1), total - largest - least * (count - 1)
    while rest > 0:
        candidates = [i for i in range(1, count) if given[i] < largest] or [i for i in range(1, count) if given[i] < bound]
        mass, remaining = sum([loads[i] for i in candidates]), rest
        for i in candidates:
            extra = min(bound - given[i], max(1, remaining * loads[i] // mass), rest)
            given[i] = given[i] + extra
            rest = rest - extra
    return np.array(given)


def gaussian(rng, shape, scale, bound, shards=(), held_as=jnp.bfloat16):
    array = jax.random.normal(rng, shape, jnp.float32) * scale
    if len(shards) > 0:
        array = block_levels(rng, shape, shards, -0.22, 0.18) * array
    return jnp.clip(array, min=-bound, max=bound).astype(held_as)


def setup_inputs(seed: int = 0) -> dict:
    seeds = jax.random.split(jax.random.key(seed), 6)
    q_of_pair_keys = jax.random.split(jax.random.fold_in(seeds[0], 1), PAIRS // P_DEV)
    q_of_pair_turns = jax.random.permutation(jax.random.fold_in(seeds[0], 3), PAIRS // P_DEV)
    q_of_pair = jax.vmap(lambda own, number: assign_block(jax.random.fold_in(seeds[0], 2), own, number, P_DEV, Q_ALL, 1, CAP, 2))(q_of_pair_keys, q_of_pair_turns).reshape((PAIRS, 1))
    q_slot = jax.random.permutation(seeds[1], Q_ALL).astype(jnp.int32)
    valence = gaussian(seeds[2], (PAIRS, NB * NB, NG), 1.0, 6.0, ((0, 16), (2, 2)))
    conduction = gaussian(seeds[3], (PAIRS, NB * NB, NG), NG ** -0.5, 0.1875, ((0, 16), (2, 2)))
    screened = gaussian(seeds[4], (Q_ALL, NG, NG), NG ** -0.5, 0.1875, ((0, 16), (1, 2)))
    return dict(q_of_pair=q_of_pair, q_slot=q_slot, valence=valence, conduction=conduction, screened=screened)


def reference(q_of_pair, q_slot, valence, conduction, screened):
    slot_index = q_slot[q_of_pair[:, 0]]
    pair_count = slot_index.shape[0]
    band_pairs = valence.shape[1]
    width = valence.shape[2]

    def block_kernel(items):
        slots, val_rows, cond_rows = items
        weights = screened[slots].astype(jnp.float32)
        applied = jnp.einsum("pgh,pbh->pbg", weights, val_rows.astype(jnp.float32))
        applied = applied.astype(jnp.bfloat16).astype(jnp.float32)
        kern = jnp.einsum("pcg,pbg->pcb", cond_rows.astype(jnp.float32), applied)
        return kern.reshape(kern.shape[0], band_pairs * band_pairs)

    result = lax.map(block_kernel, (slot_index.reshape(-1, 64),
                                    valence.reshape(-1, 64, band_pairs, width),
                                    conduction.reshape(-1, 64, band_pairs, width)))
    return result.reshape(pair_count, band_pairs * band_pairs)
```

```python
import functools

import jax
import jax.numpy as jnp
from jax import lax
from jax.experimental import pallas as pl
from jax.experimental.pallas import tpu as pltpu
from jax.sharding import PartitionSpec as P

MESH = pl.DeviceIdType.MESH


def kernel(outer, inner, local, cap, cap_pad, steps,
           source_row, target, val_hbm, cond_hbm, w_hbm, out_ref,
           val_in, cond_in, pack_v, pack_c, vbuf, cbuf, wbuf, app, part, sib, back, ret,
           in_sem, w_up, w_down, w_recv, v_send, c_send, v_recv, c_recv,
           s_send, s_recv, p_sem, r_send, r_recv):
    me = lax.axis_index("pb")
    core = lax.axis_index("ga")
    line, place = me // inner, lax.rem(me, inner)
    bands = val_in.shape[1]
    rows = cap * bands
    slots = outer * local
    half = val_in.shape[2]

    def peer(to_line, to_place):
        return (to_line * inner + to_place, core)

    sibling = (me, 1 - core)

    def slot_at(step):
        found = jnp.int32(0)
        for z in range(outer):
            for k, j in enumerate(steps[z]):
                found = jnp.where((line == z) & (step == k), jnp.int32(j), found)
        return found

    barrier = pltpu.get_barrier_semaphore()
    pl.semaphore_signal(barrier, inc=1, device_id=sibling, device_id_type=MESH)
    for d in range(1, inner):
        pl.semaphore_signal(barrier, inc=1, device_id=peer(line, lax.rem(place + d, inner)),
                            device_id_type=MESH)

    @pl.when(line > 0)
    def _():
        pl.semaphore_signal(barrier, inc=1, device_id=peer(line - 1, place), device_id_type=MESH)

    @pl.when(line < outer - 1)
    def _():
        pl.semaphore_signal(barrier, inc=1, device_id=peer(line + 1, place), device_id_type=MESH)

    copy_val = pltpu.make_async_copy(val_hbm, val_in, in_sem.at[0])
    copy_cond = pltpu.make_async_copy(cond_hbm, cond_in, in_sem.at[1])
    copy_w = pltpu.make_async_copy(w_hbm, wbuf.at[pl.ds(line * local, local)], in_sem.at[2])
    copy_w.start()
    copy_val.start()
    copy_cond.start()
    app[...] = jnp.zeros_like(app)
    copy_w.wait()
    pl.semaphore_wait(barrier, inner + (line > 0).astype(jnp.int32)
                      + (line < outer - 1).astype(jnp.int32))

    def w_copy(j, to_line, send):
        return pltpu.make_async_remote_copy(
            src_ref=wbuf.at[j], dst_ref=wbuf.at[j], send_sem=send.at[j],
            recv_sem=w_recv.at[j], device_id=peer(to_line, place), device_id_type=MESH)

    for l in range(local):
        @pl.when(line < outer - 1)
        def _():
            w_copy(line * local + l, line + 1, w_up).start()

        @pl.when(line > 0)
        def _():
            w_copy(line * local + l, line - 1, w_down).start()

    def v_copy(j, to, frm):
        return pltpu.make_async_remote_copy(
            src_ref=pack_v.at[to, j], dst_ref=vbuf.at[core, j, frm],
            send_sem=v_send.at[to * slots + j], recv_sem=v_recv.at[frm * slots + j],
            device_id=peer(line, to), device_id_type=MESH)

    def c_copy(j, to, frm):
        return pltpu.make_async_remote_copy(
            src_ref=pack_c.at[to, j], dst_ref=cbuf.at[j, frm],
            send_sem=c_send.at[to * slots + j], recv_sem=c_recv.at[frm * slots + j],
            device_id=peer(line, to), device_id_type=MESH)

    def fill(dst, src, first):
        for i in range(cap):
            dst[i * bands:(i + 1) * bands, :] = src[source_row[first + i]]

    copy_val.wait()
    copy_cond.wait()

    def pack_step(step, carry):
        j = slot_at(step)

        def pack_to(d, carry):
            to = lax.rem(place + d, inner)
            first = (to * slots + j) * cap
            fill(pack_v.at[to, j], val_in, first)
            v_copy(j, to, place).start()
            fill(pack_c.at[to, j], cond_in, first)
            c_copy(j, to, place).start()
            return carry

        lax.fori_loop(1, inner, pack_to, 0)
        first = (place * slots + j) * cap
        fill(vbuf.at[core, j, place], val_in, first)
        fill(cbuf.at[j, place], cond_in, first)
        return carry

    lax.fori_loop(0, slots, pack_step, 0)

    def w_event(t, l):
        below, above = line - t, line + t

        @pl.when(below >= 0)
        def _():
            w_copy(below * local + l, line, w_up).wait_recv()

            @pl.when(line < outer - 1)
            def _():
                w_copy(below * local + l, line + 1, w_up).start()

        @pl.when(above < outer)
        def _():
            w_copy(above * local + l, line, w_down).wait_recv()

            @pl.when(line > 0)
            def _():
                w_copy(above * local + l, line - 1, w_down).start()

    def s_copy(j):
        return pltpu.make_async_remote_copy(
            src_ref=vbuf.at[core, j], dst_ref=vbuf.at[core, j], send_sem=s_send.at[j],
            recv_sem=s_recv.at[j], device_id=sibling, device_id_type=MESH)

    def s_arrived(j):
        return pltpu.make_async_remote_copy(
            src_ref=vbuf.at[1 - core, j], dst_ref=vbuf.at[1 - core, j], send_sem=s_send.at[j],
            recv_sem=s_recv.at[j], device_id=sibling, device_id_type=MESH)

    nt = (((1,), (1,)), ((), ()))
    width = app.shape[1]
    g_all = app.shape[2]
    g_tile = min(256, g_all)
    row_pair = lax.broadcasted_iota(jnp.int32, (rows, width), 0) // bands
    col_pair = lax.broadcasted_iota(jnp.int32, (rows, width), 1) // bands
    same_pair = row_pair == col_pair
    own_lane = (lax.broadcasted_iota(jnp.int32, (cap, bands // 2, 128), 1)
                == lax.broadcasted_iota(jnp.int32, (cap, bands // 2, 128), 2) // bands)

    def compute(j):
        def apply_tile(gt, carry):
            cols = pl.ds(pl.multiple_of(gt * g_tile, g_tile), g_tile)
            total = jnp.zeros((inner * rows, g_tile), jnp.float32)
            for h in range(2):
                total = total + lax.dot_general(
                    vbuf[h, j].reshape(inner * rows, half),
                    wbuf[j, cols, h * half:(h + 1) * half], nt,
                    preferred_element_type=jnp.float32)
            app[:, 0:rows, cols] = total.astype(jnp.bfloat16).reshape(inner, rows, g_tile)
            return carry

        lax.fori_loop(0, g_all // g_tile, apply_tile, 0)

        def contract(s, carry):
            prod = lax.dot_general(cbuf[j, s], app[s], nt, preferred_element_type=jnp.float32)
            prod = jnp.where(same_pair, prod, 0.0)
            folded = prod[:, 0:128]
            for x in range(1, width // 128):
                folded = folded + prod[:, x * 128:(x + 1) * 128]
            shift = 64
            while shift >= bands:
                folded = folded + pltpu.roll(folded, shift, 1)
                shift //= 2
            folded = folded.reshape(cap, bands, 128)
            for h in range(2):
                piece = folded[:, h * (bands // 2):(h + 1) * (bands // 2), :]
                piece = jnp.sum(jnp.where(own_lane, piece, 0.0), axis=1)
                if cap_pad > cap:
                    piece = jnp.concatenate(
                        [piece, jnp.zeros((cap_pad - cap, 128), jnp.float32)], axis=0)
                part[h, s, j] = piece
            return carry

        lax.fori_loop(0, inner, contract, 0)

    events = {}
    count = (outer - 1) * local
    for e in range(count):
        events[min(slots - 1, (e + 1) * slots // count)] = (1 + e // local, e % local)

    def work(step, carry):
        for k, (t, l) in events.items():
            @pl.when(step == k)
            def _():
                w_event(t, l)

        @pl.when(step < slots)
        def _():
            j = slot_at(step)

            def take(d, carry):
                frm = lax.rem(place + d, inner)
                v_copy(j, frm, frm).wait_recv()
                return carry

            lax.fori_loop(1, inner, take, 0)
            s_copy(j).start()

        @pl.when(step > 0)
        def _():
            j = slot_at(step - 1)
            s_arrived(j).wait_recv()

            def take(d, carry):
                frm = lax.rem(place + d, inner)
                c_copy(j, frm, frm).wait_recv()
                return carry

            lax.fori_loop(1, inner, take, 0)
            compute(j)

        return carry

    lax.fori_loop(0, slots + 1, work, 0)

    p_copy = pltpu.make_async_remote_copy(
        src_ref=part.at[1 - core], dst_ref=sib, send_sem=p_sem.at[0], recv_sem=p_sem.at[1],
        device_id=sibling, device_id_type=MESH)
    p_copy.start()
    p_copy.wait_recv()

    def r_copy(to, frm):
        return pltpu.make_async_remote_copy(
            src_ref=back.at[to], dst_ref=ret.at[frm], send_sem=r_send.at[to],
            recv_sem=r_recv.at[frm], device_id=peer(line, to), device_id_type=MESH)

    def give(d, carry):
        to = lax.rem(place + d, inner)
        back[to] = (part[core, to] + sib[to]).reshape(back.shape[1:])
        r_copy(to, place).start()
        return carry

    lax.fori_loop(1, inner, give, 0)
    ret[place] = (part[core, place] + sib[place]).reshape(ret.shape[1:])

    def settle(j, carry):
        def sent(d, carry):
            to = lax.rem(place + d, inner)
            v_copy(j, to, place).wait_send()
            c_copy(j, to, place).wait_send()
            return carry

        lax.fori_loop(1, inner, sent, 0)
        s_copy(j).wait_send()

        @pl.when((line < outer - 1) & (j // local <= line))
        def _():
            w_copy(j, line + 1, w_up).wait_send()

        @pl.when((line > 0) & (j // local >= line))
        def _():
            w_copy(j, line - 1, w_down).wait_send()

        return carry

    lax.fori_loop(0, slots, settle, 0)
    p_copy.wait_send()

    def got(d, carry):
        other = lax.rem(place + d, inner)
        r_copy(other, other).wait_recv()
        r_copy(other, place).wait_send()
        return carry

    lax.fori_loop(1, inner, got, 0)

    flat = ret.reshape(ret.shape[0] * ret.shape[1], ret.shape[2])

    def place_rows(b, carry):
        for i in range(8):
            row = b * 8 + i
            out_ref[pl.ds(row, 1), :] = flat[pl.ds(target[row], 1), :]
        return carry

    lax.fori_loop(0, out_ref.shape[0] // 8, place_rows, 0)


def visit_order(outer, local):
    steps = []
    for z in range(outer):
        order = [z * local + l for l in range(local)]
        for t in range(1, outer):
            for l in range(local):
                order += [y * local + l for y in (z - t, z + t) if 0 <= y < outer]
        steps.append(order)
    return steps


def body(peer_count, q_of_pair, q_slot, valence, conduction, screened):
    pair_count, bands, half = valence.shape
    local, g_rows, g_cols = screened.shape
    q_total = q_slot.shape[0]
    cap = max(2, (3 * pair_count + 2 * q_total - 1) // (2 * q_total))
    cap_pad = -(-cap // 8) * 8
    outer = 4 if peer_count % 4 == 0 else 1
    inner = peer_count // outer
    slots = outer * local
    rows = cap * bands
    width = -(-rows // 128) * 128

    q_ids = q_of_pair[:, 0]
    q_match = q_ids[:, None] == jnp.arange(q_total, dtype=jnp.int32)[None, :]
    slot_index = jnp.sum(jnp.where(q_match, q_slot[None, :], 0), axis=1)
    order_row = jnp.arange(pair_count, dtype=jnp.int32)
    same_q = (q_ids[:, None] == q_ids[None, :]) & (order_row[None, :] < order_row[:, None])
    rank = jnp.sum(same_q.astype(jnp.int32), axis=1)
    owner = slot_index // local
    group = owner % inner * slots + owner // inner * local + slot_index % local
    packed = group * cap + rank
    target = group * cap_pad + rank
    hit = packed[None, :] == jnp.arange(inner * slots * cap, dtype=jnp.int32)[:, None]
    source_row = jnp.sum(jnp.where(hit, order_row[None, :], 0), axis=1)

    smem = pl.BlockSpec(memory_space=pltpu.SMEM)
    anywhere = pl.BlockSpec(memory_space=pl.ANY)
    dma = pltpu.SemaphoreType.DMA
    bf16, f32 = jnp.bfloat16, jnp.float32
    return pl.pallas_call(
        functools.partial(kernel, outer, inner, local, cap, cap_pad, visit_order(outer, local)),
        out_shape=jax.ShapeDtypeStruct((pair_count, bands * bands // 2), f32),
        in_specs=[smem, smem, anywhere, anywhere, anywhere],
        out_specs=pl.BlockSpec(memory_space=pltpu.VMEM),
        scratch_shapes=[
            pltpu.VMEM((pair_count, bands, half), bf16),
            pltpu.VMEM((pair_count, bands, half), bf16),
            pltpu.VMEM((inner, slots, rows, half), bf16),
            pltpu.VMEM((inner, slots, rows, half), bf16),
            pltpu.VMEM((2, slots, inner, rows, half), bf16),
            pltpu.VMEM((slots, inner, rows, half), bf16),
            pltpu.VMEM((slots, g_rows, g_cols), bf16),
            pltpu.VMEM((inner, width, g_rows), bf16),
            pltpu.VMEM((2, inner, slots, cap_pad, 128), f32),
            pltpu.VMEM((inner, slots, cap_pad, 128), f32),
            pltpu.VMEM((inner, slots * cap_pad, 128), f32),
            pltpu.VMEM((inner, slots * cap_pad, 128), f32),
            dma((3,)), dma((slots,)), dma((slots,)), dma((slots,)),
            dma((inner * slots,)), dma((inner * slots,)),
            dma((inner * slots,)), dma((inner * slots,)),
            dma((slots,)), dma((slots,)), dma((2,)), dma((inner,)), dma((inner,)),
        ],
        compiler_params=pltpu.CompilerParams(
            collective_id=0, has_side_effects=True, vmem_limit_bytes=58 * 1024 * 1024),
        cost_estimate=pl.CostEstimate(
            flops=2 * inner * slots * rows * g_rows * g_cols, transcendentals=0,
            bytes_accessed=4 * pair_count * bands * half + 2 * local * g_rows * g_cols),
    )(source_row, target, valence, conduction, screened)


def solution(mesh):
    in_specs = (P("pb", None), P(), P("pb", None, "ga"), P("pb", None, "ga"), P("pb", "ga", None))
    return jax.shard_map(functools.partial(body, mesh.shape["pb"]), mesh=mesh, in_specs=in_specs,
                         out_specs=P("pb", "ga"), check_vma=False)
```

```python
import functools

import jax
import jax.numpy as jnp
from jax import lax
from jax.experimental import pallas as pl
from jax.experimental.pallas import tpu as pltpu
from jax.sharding import PartitionSpec as P

MESH = pl.DeviceIdType.MESH
WINDOW = 3


def kernel(outer, inner, local, cap, cap_pad, steps,
           source_row, target, val_hbm, cond_hbm, w_hbm, out_ref,
           val_in, cond_in, pack_v, pack_c, vbuf, cbuf, wbuf, app, part, sib, back, ret,
           in_sem, w_up, w_down, w_recv, v_send, c_send, v_recv, c_recv,
           s_send, s_recv, p_send, p_recv, r_send, r_recv):
    me = lax.axis_index("pb")
    core = lax.axis_index("ga")
    line, place = me // inner, lax.rem(me, inner)
    bands = val_in.shape[1]
    rows = cap * bands
    slots = outer * local
    half = val_in.shape[2]

    def peer(to_line, to_place):
        return (to_line * inner + to_place, core)

    sibling = (me, 1 - core)

    def slot_at(step):
        found = jnp.int32(0)
        for z in range(outer):
            for k, j in enumerate(steps[z]):
                found = jnp.where((line == z) & (step == k), jnp.int32(j), found)
        return found

    barrier = pltpu.get_barrier_semaphore()
    pl.semaphore_signal(barrier, inc=1, device_id=sibling, device_id_type=MESH)
    for d in range(1, inner):
        pl.semaphore_signal(barrier, inc=1, device_id=peer(line, lax.rem(place + d, inner)),
                            device_id_type=MESH)

    @pl.when(line > 0)
    def _():
        pl.semaphore_signal(barrier, inc=1, device_id=peer(line - 1, place), device_id_type=MESH)

    @pl.when(line < outer - 1)
    def _():
        pl.semaphore_signal(barrier, inc=1, device_id=peer(line + 1, place), device_id_type=MESH)

    copy_val = pltpu.make_async_copy(val_hbm, val_in, in_sem.at[0])
    copy_cond = pltpu.make_async_copy(cond_hbm, cond_in, in_sem.at[1])
    copy_w = pltpu.make_async_copy(w_hbm, wbuf.at[pl.ds(line * local, local)], in_sem.at[2])
    copy_val.start()
    copy_cond.start()
    copy_w.start()
    app[...] = jnp.zeros_like(app)
    pl.semaphore_wait(barrier, inner + (line > 0).astype(jnp.int32)
                      + (line < outer - 1).astype(jnp.int32))

    def w_copy(j, to_line, send):
        return pltpu.make_async_remote_copy(
            src_ref=wbuf.at[j], dst_ref=wbuf.at[j], send_sem=send.at[j],
            recv_sem=w_recv.at[j], device_id=peer(to_line, place), device_id_type=MESH)

    def send_own(l):
        def own_copy(to_line, send):
            return pltpu.make_async_remote_copy(
                src_ref=w_hbm.at[l], dst_ref=wbuf.at[line * local + l],
                send_sem=send.at[line * local + l], recv_sem=w_recv.at[line * local + l],
                device_id=peer(to_line, place), device_id_type=MESH)

        @pl.when(line < outer - 1)
        def _():
            own_copy(line + 1, w_up).start()

        @pl.when(line > 0)
        def _():
            own_copy(line - 1, w_down).start()

    send_own(0)

    def v_copy(j, to, frm):
        return pltpu.make_async_remote_copy(
            src_ref=pack_v.at[to, j], dst_ref=vbuf.at[core, j, frm],
            send_sem=v_send.at[to * slots + j], recv_sem=v_recv.at[frm * slots + j],
            device_id=peer(line, to), device_id_type=MESH)

    def c_copy(j, to, frm):
        return pltpu.make_async_remote_copy(
            src_ref=pack_c.at[to, j], dst_ref=cbuf.at[j, frm],
            send_sem=c_send.at[to * slots + j], recv_sem=c_recv.at[frm * slots + j],
            device_id=peer(line, to), device_id_type=MESH)

    def fill(dst, src, first):
        for i in range(cap):
            dst[i * bands:(i + 1) * bands, :] = src[source_row[first + i]]

    copy_val.wait()
    copy_cond.wait()

    def pack_step(step, carry):
        j = slot_at(step)

        def pack_to(d, carry):
            to = lax.rem(place + d, inner)
            first = (to * slots + j) * cap
            fill(pack_v.at[to, j], val_in, first)
            v_copy(j, to, place).start()
            fill(pack_c.at[to, j], cond_in, first)
            c_copy(j, to, place).start()
            return carry

        lax.fori_loop(1, inner, pack_to, 0)
        first = (place * slots + j) * cap
        fill(vbuf.at[core, j, place], val_in, first)
        fill(cbuf.at[j, place], cond_in, first)
        return carry

    lax.fori_loop(0, WINDOW, pack_step, 0)
    copy_w.wait()

    def w_event(t, l):
        below, above = line - t, line + t

        @pl.when(below >= 0)
        def _():
            w_copy(below * local + l, line, w_up).wait_recv()

            @pl.when(line < outer - 1)
            def _():
                w_copy(below * local + l, line + 1, w_up).start()

        @pl.when(above < outer)
        def _():
            w_copy(above * local + l, line, w_down).wait_recv()

            @pl.when(line > 0)
            def _():
                w_copy(above * local + l, line - 1, w_down).start()

    def s_copy(j):
        return pltpu.make_async_remote_copy(
            src_ref=vbuf.at[core, j], dst_ref=vbuf.at[core, j], send_sem=s_send.at[j],
            recv_sem=s_recv.at[j], device_id=sibling, device_id_type=MESH)

    def s_arrived(j):
        return pltpu.make_async_remote_copy(
            src_ref=vbuf.at[1 - core, j], dst_ref=vbuf.at[1 - core, j], send_sem=s_send.at[j],
            recv_sem=s_recv.at[j], device_id=sibling, device_id_type=MESH)

    nt = (((1,), (1,)), ((), ()))
    width = app.shape[1]
    g_all = app.shape[2]
    g_tile = min(256, g_all)
    row_pair = lax.broadcasted_iota(jnp.int32, (rows, width), 0) // bands
    col_pair = lax.broadcasted_iota(jnp.int32, (rows, width), 1) // bands
    same_pair = row_pair == col_pair
    own_lane = (lax.broadcasted_iota(jnp.int32, (cap, bands // 2, 128), 1)
                == lax.broadcasted_iota(jnp.int32, (cap, bands // 2, 128), 2) // bands)

    def compute(j):
        def apply_tile(gt, carry):
            cols = pl.ds(pl.multiple_of(gt * g_tile, g_tile), g_tile)
            total = jnp.zeros((inner * rows, g_tile), jnp.float32)
            for h in range(2):
                total = total + lax.dot_general(
                    vbuf[h, j].reshape(inner * rows, half),
                    wbuf[j, cols, h * half:(h + 1) * half], nt,
                    preferred_element_type=jnp.float32)
            app[:, 0:rows, cols] = total.astype(jnp.bfloat16).reshape(inner, rows, g_tile)
            return carry

        lax.fori_loop(0, g_all // g_tile, apply_tile, 0)

        def contract(s, carry):
            prod = lax.dot_general(cbuf[j, s], app[s], nt, preferred_element_type=jnp.float32)
            prod = jnp.where(same_pair, prod, 0.0)
            folded = prod[:, 0:128]
            for x in range(1, width // 128):
                folded = folded + prod[:, x * 128:(x + 1) * 128]
            shift = 64
            while shift >= bands:
                folded = folded + pltpu.roll(folded, shift, 1)
                shift //= 2
            folded = folded.reshape(cap, bands, 128)
            for h in range(2):
                piece = folded[:, h * (bands // 2):(h + 1) * (bands // 2), :]
                piece = jnp.sum(jnp.where(own_lane, piece, 0.0), axis=1)
                if cap_pad > cap:
                    piece = jnp.concatenate(
                        [piece, jnp.zeros((cap_pad - cap, 128), jnp.float32)], axis=0)
                part[h, j, s] = piece
            return carry

        lax.fori_loop(0, inner, contract, 0)

    events = {}
    count = (outer - 1) * local
    for e in range(count):
        events[1 + e * (slots + 1) // count] = (1 + e // local, e % local)

    def p_copy(j):
        return pltpu.make_async_remote_copy(
            src_ref=part.at[1 - core, j], dst_ref=sib.at[j], send_sem=p_send.at[j],
            recv_sem=p_recv.at[j], device_id=sibling, device_id_type=MESH)

    def r_copy(j, to, frm):
        return pltpu.make_async_remote_copy(
            src_ref=back.at[to, j], dst_ref=ret.at[frm, j], send_sem=r_send.at[to * slots + j],
            recv_sem=r_recv.at[frm * slots + j], device_id=peer(line, to), device_id_type=MESH)

    def work(step, carry):
        @pl.when(step < slots)
        def _():
            j = slot_at(step)

            def take(d, carry):
                frm = lax.rem(place + d, inner)
                v_copy(j, frm, frm).wait_recv()
                return carry

            lax.fori_loop(1, inner, take, 0)
            s_copy(j).start()

        for l in range(1, local):
            @pl.when(step == l - 1)
            def _():
                send_own(l)

        @pl.when(step + WINDOW < slots)
        def _():
            pack_step(step + WINDOW, 0)

        for k, (t, l) in events.items():
            @pl.when(step == k)
            def _():
                w_event(t, l)

        @pl.when(step > 1)
        def _():
            j = slot_at(step - 2)
            p_copy(j).wait_recv()

            def give(d, carry):
                to = lax.rem(place + d, inner)
                back[to, j] = part[core, j, to] + sib[j, to]
                r_copy(j, to, place).start()
                return carry

            lax.fori_loop(1, inner, give, 0)
            ret[place, j] = part[core, j, place] + sib[j, place]

        @pl.when((step > 0) & (step <= slots))
        def _():
            j = slot_at(step - 1)
            s_arrived(j).wait_recv()

            def take(d, carry):
                frm = lax.rem(place + d, inner)
                c_copy(j, frm, frm).wait_recv()
                return carry

            lax.fori_loop(1, inner, take, 0)
            compute(j)
            p_copy(j).start()

        return carry

    lax.fori_loop(0, slots + 2, work, 0)

    def settle(j, carry):
        def sent(d, carry):
            to = lax.rem(place + d, inner)
            v_copy(j, to, place).wait_send()
            c_copy(j, to, place).wait_send()
            return carry

        lax.fori_loop(1, inner, sent, 0)
        s_copy(j).wait_send()
        p_copy(j).wait_send()

        @pl.when((line < outer - 1) & (j // local <= line))
        def _():
            w_copy(j, line + 1, w_up).wait_send()

        @pl.when((line > 0) & (j // local >= line))
        def _():
            w_copy(j, line - 1, w_down).wait_send()

        return carry

    lax.fori_loop(0, slots, settle, 0)

    def got(j, carry):
        def each(d, carry):
            other = lax.rem(place + d, inner)
            r_copy(j, other, other).wait_recv()
            r_copy(j, other, place).wait_send()
            return carry

        return lax.fori_loop(1, inner, each, carry)

    lax.fori_loop(0, slots, got, 0)

    flat = ret.reshape(inner * slots * cap_pad, 128)

    def place_rows(b, carry):
        for i in range(8):
            row = b * 8 + i
            out_ref[pl.ds(row, 1), :] = flat[pl.ds(target[row], 1), :]
        return carry

    lax.fori_loop(0, out_ref.shape[0] // 8, place_rows, 0)


def visit_order(outer, local):
    steps = []
    for z in range(outer):
        order = [z * local + l for l in range(local)]
        for t in range(1, outer):
            for l in range(local):
                order += [y * local + l for y in (z - t, z + t) if 0 <= y < outer]
        steps.append(order)
    return steps


def body(peer_count, q_of_pair, q_slot, valence, conduction, screened):
    pair_count, bands, half = valence.shape
    local, g_rows, g_cols = screened.shape
    q_total = q_slot.shape[0]
    cap = max(2, (3 * pair_count + 2 * q_total - 1) // (2 * q_total))
    cap_pad = -(-cap // 8) * 8
    outer = 4 if peer_count % 4 == 0 else 1
    inner = peer_count // outer
    slots = outer * local
    rows = cap * bands
    width = -(-rows // 128) * 128

    q_ids = q_of_pair[:, 0]
    q_match = q_ids[:, None] == jnp.arange(q_total, dtype=jnp.int32)[None, :]
    slot_index = jnp.sum(jnp.where(q_match, q_slot[None, :], 0), axis=1)
    order_row = jnp.arange(pair_count, dtype=jnp.int32)
    same_q = (q_ids[:, None] == q_ids[None, :]) & (order_row[None, :] < order_row[:, None])
    rank = jnp.sum(same_q.astype(jnp.int32), axis=1)
    owner = slot_index // local
    group = owner % inner * slots + owner // inner * local + slot_index % local
    packed = group * cap + rank
    target = group * cap_pad + rank
    hit = packed[None, :] == jnp.arange(inner * slots * cap, dtype=jnp.int32)[:, None]
    source_row = jnp.sum(jnp.where(hit, order_row[None, :], 0), axis=1)

    smem = pl.BlockSpec(memory_space=pltpu.SMEM)
    anywhere = pl.BlockSpec(memory_space=pl.ANY)
    dma = pltpu.SemaphoreType.DMA
    bf16, f32 = jnp.bfloat16, jnp.float32
    return pl.pallas_call(
        functools.partial(kernel, outer, inner, local, cap, cap_pad, visit_order(outer, local)),
        out_shape=jax.ShapeDtypeStruct((pair_count, bands * bands // 2), f32),
        in_specs=[smem, smem, anywhere, anywhere, anywhere],
        out_specs=pl.BlockSpec(memory_space=pltpu.VMEM),
        scratch_shapes=[
            pltpu.VMEM((pair_count, bands, half), bf16),
            pltpu.VMEM((pair_count, bands, half), bf16),
            pltpu.VMEM((inner, slots, rows, half), bf16),
            pltpu.VMEM((inner, slots, rows, half), bf16),
            pltpu.VMEM((2, slots, inner, rows, half), bf16),
            pltpu.VMEM((slots, inner, rows, half), bf16),
            pltpu.VMEM((slots, g_rows, g_cols), bf16),
            pltpu.VMEM((inner, width, g_rows), bf16),
            pltpu.VMEM((2, slots, inner, cap_pad, 128), f32),
            pltpu.VMEM((slots, inner, cap_pad, 128), f32),
            pltpu.VMEM((inner, slots, cap_pad, 128), f32),
            pltpu.VMEM((inner, slots, cap_pad, 128), f32),
            dma((3,)), dma((slots,)), dma((slots,)), dma((slots,)),
            dma((inner * slots,)), dma((inner * slots,)),
            dma((inner * slots,)), dma((inner * slots,)),
            dma((slots,)), dma((slots,)), dma((slots,)), dma((slots,)),
            dma((inner * slots,)), dma((inner * slots,)),
        ],
        compiler_params=pltpu.CompilerParams(
            collective_id=0, has_side_effects=True, vmem_limit_bytes=58 * 1024 * 1024),
        cost_estimate=pl.CostEstimate(
            flops=2 * inner * slots * rows * g_rows * g_cols, transcendentals=0,
            bytes_accessed=4 * pair_count * bands * half + 2 * local * g_rows * g_cols),
    )(source_row, target, valence, conduction, screened)


def solution(mesh):
    in_specs = (P("pb", None), P(), P("pb", None, "ga"), P("pb", None, "ga"), P("pb", "ga", None))
    return jax.shard_map(functools.partial(body, mesh.shape["pb"]), mesh=mesh, in_specs=in_specs,
                         out_specs=P("pb", "ga"), check_vma=False)
```

```python
import functools

import jax
import jax.numpy as jnp
from jax import lax
from jax.experimental import pallas as pl
from jax.experimental.pallas import tpu as pltpu
from jax.sharding import PartitionSpec as P

MESH = pl.DeviceIdType.MESH
WINDOW = 3


def kernel(outer, inner, local, cap, cap_pad, steps,
           source_row, target, val_hbm, cond_hbm, w_hbm, out_ref,
           val_in, cond_in, pack_v, pack_c, vbuf, cbuf, wbuf, app, part, sib, back, ret,
           in_sem, w_up, w_down, w_recv, v_send, c_send, v_recv, c_recv,
           s_send, s_recv, p_send, p_recv, r_send, r_recv):
    me = lax.axis_index("pb")
    core = lax.axis_index("ga")
    line, place = me // inner, lax.rem(me, inner)
    bands = val_in.shape[1]
    rows = cap * bands
    slots = outer * local
    half = val_in.shape[2]

    def peer(to_line, to_place):
        return (to_line * inner + to_place, core)

    sibling = (me, 1 - core)

    def slot_at(step):
        found = jnp.int32(0)
        for z in range(outer):
            for k, j in enumerate(steps[z]):
                found = jnp.where((line == z) & (step == k), jnp.int32(j), found)
        return found

    barrier = pltpu.get_barrier_semaphore()
    pl.semaphore_signal(barrier, inc=1, device_id=sibling, device_id_type=MESH)
    for d in range(1, inner):
        pl.semaphore_signal(barrier, inc=1, device_id=peer(line, lax.rem(place + d, inner)),
                            device_id_type=MESH)

    @pl.when(line > 0)
    def _():
        pl.semaphore_signal(barrier, inc=1, device_id=peer(line - 1, place), device_id_type=MESH)

    @pl.when(line < outer - 1)
    def _():
        pl.semaphore_signal(barrier, inc=1, device_id=peer(line + 1, place), device_id_type=MESH)

    copy_val = pltpu.make_async_copy(val_hbm, val_in, in_sem.at[0])
    copy_cond = pltpu.make_async_copy(cond_hbm, cond_in, in_sem.at[1])
    copy_w = pltpu.make_async_copy(w_hbm, wbuf.at[pl.ds(line * local, local)], in_sem.at[2])
    copy_val.start()
    app[...] = jnp.zeros_like(app)
    pl.semaphore_wait(barrier, inner + (line > 0).astype(jnp.int32)
                      + (line < outer - 1).astype(jnp.int32))

    def w_copy(j, to_line, send):
        return pltpu.make_async_remote_copy(
            src_ref=wbuf.at[j], dst_ref=wbuf.at[j], send_sem=send.at[j],
            recv_sem=w_recv.at[j], device_id=peer(to_line, place), device_id_type=MESH)

    def send_own(l):
        def own_copy(to_line, send):
            return pltpu.make_async_remote_copy(
                src_ref=w_hbm.at[l], dst_ref=wbuf.at[line * local + l],
                send_sem=send.at[line * local + l], recv_sem=w_recv.at[line * local + l],
                device_id=peer(to_line, place), device_id_type=MESH)

        @pl.when(line < outer - 1)
        def _():
            own_copy(line + 1, w_up).start()

        @pl.when(line > 0)
        def _():
            own_copy(line - 1, w_down).start()

    send_own(0)

    def v_copy(j, to, frm):
        return pltpu.make_async_remote_copy(
            src_ref=pack_v.at[to, j], dst_ref=vbuf.at[core, j, frm],
            send_sem=v_send.at[to * slots + j], recv_sem=v_recv.at[frm * slots + j],
            device_id=peer(line, to), device_id_type=MESH)

    def c_copy(j, to, frm):
        return pltpu.make_async_remote_copy(
            src_ref=pack_c.at[to, j], dst_ref=cbuf.at[j, frm],
            send_sem=c_send.at[to * slots + j], recv_sem=c_recv.at[frm * slots + j],
            device_id=peer(line, to), device_id_type=MESH)

    def fill(dst, src, first):
        for i in range(cap):
            dst[i * bands:(i + 1) * bands, :] = src[source_row[first + i]]

    def pack_val(j):
        def pack_to(d, carry):
            to = lax.rem(place + d, inner)
            fill(pack_v.at[to, j], val_in, (to * slots + j) * cap)
            v_copy(j, to, place).start()
            return carry

        lax.fori_loop(1, inner, pack_to, 0)
        fill(vbuf.at[core, j, place], val_in, (place * slots + j) * cap)

    def pack_cond(j):
        def pack_to(d, carry):
            to = lax.rem(place + d, inner)
            fill(pack_c.at[to, j], cond_in, (to * slots + j) * cap)
            c_copy(j, to, place).start()
            return carry

        lax.fori_loop(1, inner, pack_to, 0)
        fill(cbuf.at[j, place], cond_in, (place * slots + j) * cap)

    def pack_step(step, carry):
        j = slot_at(step)
        pack_val(j)
        pack_cond(j)
        return carry

    copy_val.wait()
    copy_cond.start()
    copy_w.start()
    pack_val(slot_at(0))
    copy_cond.wait()
    pack_cond(slot_at(0))
    lax.fori_loop(1, WINDOW, pack_step, 0)
    copy_w.wait()

    def w_event(t, l):
        below, above = line - t, line + t

        @pl.when(below >= 0)
        def _():
            w_copy(below * local + l, line, w_up).wait_recv()

            @pl.when(line < outer - 1)
            def _():
                w_copy(below * local + l, line + 1, w_up).start()

        @pl.when(above < outer)
        def _():
            w_copy(above * local + l, line, w_down).wait_recv()

            @pl.when(line > 0)
            def _():
                w_copy(above * local + l, line - 1, w_down).start()

    def s_copy(j):
        return pltpu.make_async_remote_copy(
            src_ref=vbuf.at[core, j], dst_ref=vbuf.at[core, j], send_sem=s_send.at[j],
            recv_sem=s_recv.at[j], device_id=sibling, device_id_type=MESH)

    def s_arrived(j):
        return pltpu.make_async_remote_copy(
            src_ref=vbuf.at[1 - core, j], dst_ref=vbuf.at[1 - core, j], send_sem=s_send.at[j],
            recv_sem=s_recv.at[j], device_id=sibling, device_id_type=MESH)

    nt = (((1,), (1,)), ((), ()))
    width = app.shape[1]
    g_all = app.shape[2]
    g_tile = min(256, g_all)
    row_pair = lax.broadcasted_iota(jnp.int32, (rows, width), 0) // bands
    col_pair = lax.broadcasted_iota(jnp.int32, (rows, width), 1) // bands
    same_pair = row_pair == col_pair
    own_lane = (lax.broadcasted_iota(jnp.int32, (cap, bands // 2, 128), 1)
                == lax.broadcasted_iota(jnp.int32, (cap, bands // 2, 128), 2) // bands)

    def compute(j):
        def apply_tile(gt, carry):
            cols = pl.ds(pl.multiple_of(gt * g_tile, g_tile), g_tile)
            total = jnp.zeros((inner * rows, g_tile), jnp.float32)
            for h in range(2):
                total = total + lax.dot_general(
                    vbuf[h, j].reshape(inner * rows, half),
                    wbuf[j, cols, h * half:(h + 1) * half], nt,
                    preferred_element_type=jnp.float32)
            app[:, 0:rows, cols] = total.astype(jnp.bfloat16).reshape(inner, rows, g_tile)
            return carry

        lax.fori_loop(0, g_all // g_tile, apply_tile, 0)

        def take(d, carry):
            frm = lax.rem(place + d, inner)
            c_copy(j, frm, frm).wait_recv()
            return carry

        lax.fori_loop(1, inner, take, 0)

        def contract(s, carry):
            prod = lax.dot_general(cbuf[j, s], app[s], nt, preferred_element_type=jnp.float32)
            prod = jnp.where(same_pair, prod, 0.0)
            folded = prod[:, 0:128]
            for x in range(1, width // 128):
                folded = folded + prod[:, x * 128:(x + 1) * 128]
            shift = 64
            while shift >= bands:
                folded = folded + pltpu.roll(folded, shift, 1)
                shift //= 2
            folded = folded.reshape(cap, bands, 128)
            for h in range(2):
                piece = folded[:, h * (bands // 2):(h + 1) * (bands // 2), :]
                piece = jnp.sum(jnp.where(own_lane, piece, 0.0), axis=1)
                if cap_pad > cap:
                    piece = jnp.concatenate(
                        [piece, jnp.zeros((cap_pad - cap, 128), jnp.float32)], axis=0)
                part[h, j, s] = piece
            return carry

        lax.fori_loop(0, inner, contract, 0)

    events = {}
    count = (outer - 1) * local
    for e in range(count):
        events[1 + e * (slots + 1) // count] = (1 + e // local, e % local)

    def p_copy(j):
        return pltpu.make_async_remote_copy(
            src_ref=part.at[1 - core, j], dst_ref=sib.at[j], send_sem=p_send.at[j],
            recv_sem=p_recv.at[j], device_id=sibling, device_id_type=MESH)

    def r_copy(j, to, frm):
        return pltpu.make_async_remote_copy(
            src_ref=back.at[to, j], dst_ref=ret.at[frm, j], send_sem=r_send.at[to * slots + j],
            recv_sem=r_recv.at[frm * slots + j], device_id=peer(line, to), device_id_type=MESH)

    def work(step, carry):
        @pl.when(step < slots)
        def _():
            j = slot_at(step)

            def take(d, carry):
                frm = lax.rem(place + d, inner)
                v_copy(j, frm, frm).wait_recv()
                return carry

            lax.fori_loop(1, inner, take, 0)
            s_copy(j).start()

        for l in range(1, local):
            @pl.when(step == l - 1)
            def _():
                send_own(l)

        @pl.when(step + WINDOW < slots)
        def _():
            pack_step(step + WINDOW, 0)

        for k, (t, l) in events.items():
            @pl.when(step == k)
            def _():
                w_event(t, l)

        @pl.when(step > 1)
        def _():
            j = slot_at(step - 2)
            p_copy(j).wait_recv()

            def give(d, carry):
                to = lax.rem(place + d, inner)
                back[to, j] = part[core, j, to] + sib[j, to]
                r_copy(j, to, place).start()
                return carry

            lax.fori_loop(1, inner, give, 0)
            ret[place, j] = part[core, j, place] + sib[j, place]

        @pl.when((step > 0) & (step <= slots))
        def _():
            j = slot_at(step - 1)
            s_arrived(j).wait_recv()

            compute(j)
            p_copy(j).start()

        return carry

    lax.fori_loop(0, slots + 2, work, 0)

    def settle(j, carry):
        def sent(d, carry):
            to = lax.rem(place + d, inner)
            v_copy(j, to, place).wait_send()
            c_copy(j, to, place).wait_send()
            return carry

        lax.fori_loop(1, inner, sent, 0)
        s_copy(j).wait_send()
        p_copy(j).wait_send()

        @pl.when((line < outer - 1) & (j // local <= line))
        def _():
            w_copy(j, line + 1, w_up).wait_send()

        @pl.when((line > 0) & (j // local >= line))
        def _():
            w_copy(j, line - 1, w_down).wait_send()

        return carry

    lax.fori_loop(0, slots, settle, 0)

    def got(j, carry):
        def each(d, carry):
            other = lax.rem(place + d, inner)
            r_copy(j, other, other).wait_recv()
            r_copy(j, other, place).wait_send()
            return carry

        return lax.fori_loop(1, inner, each, carry)

    lax.fori_loop(0, slots, got, 0)

    flat = ret.reshape(inner * slots * cap_pad, 128)

    def place_rows(b, carry):
        for i in range(8):
            row = b * 8 + i
            out_ref[pl.ds(row, 1), :] = flat[pl.ds(target[row], 1), :]
        return carry

    lax.fori_loop(0, out_ref.shape[0] // 8, place_rows, 0)


def visit_order(outer, local):
    steps = []
    for z in range(outer):
        order = [z * local + l for l in range(local)]
        for t in range(1, outer):
            for l in range(local):
                order += [y * local + l for y in (z - t, z + t) if 0 <= y < outer]
        steps.append(order)
    return steps


def body(peer_count, q_of_pair, q_slot, valence, conduction, screened):
    pair_count, bands, half = valence.shape
    local, g_rows, g_cols = screened.shape
    q_total = q_slot.shape[0]
    cap = max(2, (3 * pair_count + 2 * q_total - 1) // (2 * q_total))
    cap_pad = -(-cap // 8) * 8
    outer = 4 if peer_count % 4 == 0 else 1
    inner = peer_count // outer
    slots = outer * local
    rows = cap * bands
    width = -(-rows // 128) * 128

    q_ids = q_of_pair[:, 0]
    q_match = q_ids[:, None] == jnp.arange(q_total, dtype=jnp.int32)[None, :]
    slot_index = jnp.sum(jnp.where(q_match, q_slot[None, :], 0), axis=1)
    order_row = jnp.arange(pair_count, dtype=jnp.int32)
    same_q = (q_ids[:, None] == q_ids[None, :]) & (order_row[None, :] < order_row[:, None])
    rank = jnp.sum(same_q.astype(jnp.int32), axis=1)
    owner = slot_index // local
    group = owner % inner * slots + owner // inner * local + slot_index % local
    packed = group * cap + rank
    target = group * cap_pad + rank
    hit = packed[None, :] == jnp.arange(inner * slots * cap, dtype=jnp.int32)[:, None]
    source_row = jnp.sum(jnp.where(hit, order_row[None, :], 0), axis=1)

    smem = pl.BlockSpec(memory_space=pltpu.SMEM)
    anywhere = pl.BlockSpec(memory_space=pl.ANY)
    dma = pltpu.SemaphoreType.DMA
    bf16, f32 = jnp.bfloat16, jnp.float32
    return pl.pallas_call(
        functools.partial(kernel, outer, inner, local, cap, cap_pad, visit_order(outer, local)),
        out_shape=jax.ShapeDtypeStruct((pair_count, bands * bands // 2), f32),
        in_specs=[smem, smem, anywhere, anywhere, anywhere],
        out_specs=pl.BlockSpec(memory_space=pltpu.VMEM),
        scratch_shapes=[
            pltpu.VMEM((pair_count, bands, half), bf16),
            pltpu.VMEM((pair_count, bands, half), bf16),
            pltpu.VMEM((inner, slots, rows, half), bf16),
            pltpu.VMEM((inner, slots, rows, half), bf16),
            pltpu.VMEM((2, slots, inner, rows, half), bf16),
            pltpu.VMEM((slots, inner, rows, half), bf16),
            pltpu.VMEM((slots, g_rows, g_cols), bf16),
            pltpu.VMEM((inner, width, g_rows), bf16),
            pltpu.VMEM((2, slots, inner, cap_pad, 128), f32),
            pltpu.VMEM((slots, inner, cap_pad, 128), f32),
            pltpu.VMEM((inner, slots, cap_pad, 128), f32),
            pltpu.VMEM((inner, slots, cap_pad, 128), f32),
            dma((3,)), dma((slots,)), dma((slots,)), dma((slots,)),
            dma((inner * slots,)), dma((inner * slots,)),
            dma((inner * slots,)), dma((inner * slots,)),
            dma((slots,)), dma((slots,)), dma((slots,)), dma((slots,)),
            dma((inner * slots,)), dma((inner * slots,)),
        ],
        compiler_params=pltpu.CompilerParams(
            collective_id=0, has_side_effects=True, vmem_limit_bytes=58 * 1024 * 1024),
        cost_estimate=pl.CostEstimate(
            flops=2 * inner * slots * rows * g_rows * g_cols, transcendentals=0,
            bytes_accessed=4 * pair_count * bands * half + 2 * local * g_rows * g_cols),
    )(source_row, target, valence, conduction, screened)


def solution(mesh):
    in_specs = (P("pb", None), P(), P("pb", None, "ga"), P("pb", None, "ga"), P("pb", "ga", None))
    return jax.shard_map(functools.partial(body, mesh.shape["pb"]), mesh=mesh, in_specs=in_specs,
                         out_specs=P("pb", "ga"), check_vma=False)
```

```python
import functools

import jax
import jax.numpy as jnp
from jax import lax
from jax.experimental import pallas as pl
from jax.experimental.pallas import tpu as pltpu
from jax.sharding import PartitionSpec as P

MESH = pl.DeviceIdType.MESH
WINDOW = 4


def kernel(outer, inner, local, cap, cap_pad, steps,
           source_row, target, val_hbm, cond_hbm, w_hbm, out_ref,
           val_in, cond_in, pack_v, pack_c, vbuf, cbuf, wbuf, hop_v, hop_c, app, part, sib, back, ret,
           in_sem, w_up, w_down, w_recv, v_send, c_send, v_recv, c_recv,
           s_send, s_recv, p_send, p_recv, r_send, r_recv, hop_send, hop_recv):
    me = lax.axis_index("pb")
    core = lax.axis_index("ga")
    line, place = me // inner, lax.rem(me, inner)
    bands = val_in.shape[1]
    rows = cap * bands
    slots = outer * local
    half = val_in.shape[2]

    def peer(to_line, to_place):
        return (to_line * inner + to_place, core)

    sibling = (me, 1 - core)

    def slot_at(step):
        found = jnp.int32(0)
        for z in range(outer):
            for k, j in enumerate(steps[z]):
                found = jnp.where((line == z) & (step == k), jnp.int32(j), found)
        return found

    barrier = pltpu.get_barrier_semaphore()
    pl.semaphore_signal(barrier, inc=1, device_id=sibling, device_id_type=MESH)
    for d in range(1, inner):
        pl.semaphore_signal(barrier, inc=1, device_id=peer(line, lax.rem(place + d, inner)),
                            device_id_type=MESH)

    @pl.when(line > 0)
    def _():
        pl.semaphore_signal(barrier, inc=1, device_id=peer(line - 1, place), device_id_type=MESH)

    @pl.when(line < outer - 1)
    def _():
        pl.semaphore_signal(barrier, inc=1, device_id=peer(line + 1, place), device_id_type=MESH)

    copy_val = pltpu.make_async_copy(val_hbm, val_in, in_sem.at[0])
    copy_cond = pltpu.make_async_copy(cond_hbm, cond_in, in_sem.at[1])
    copy_w = pltpu.make_async_copy(w_hbm, wbuf.at[pl.ds(line * local, local)], in_sem.at[2])
    copy_val.start()
    app[...] = jnp.zeros_like(app)
    pl.semaphore_wait(barrier, inner + (line > 0).astype(jnp.int32)
                      + (line < outer - 1).astype(jnp.int32))

    def w_copy(j, to_line, send):
        return pltpu.make_async_remote_copy(
            src_ref=wbuf.at[j], dst_ref=wbuf.at[j], send_sem=send.at[j],
            recv_sem=w_recv.at[j], device_id=peer(to_line, place), device_id_type=MESH)

    def send_own(l):
        def own_copy(to_line, send):
            return pltpu.make_async_remote_copy(
                src_ref=w_hbm.at[l], dst_ref=wbuf.at[line * local + l],
                send_sem=send.at[line * local + l], recv_sem=w_recv.at[line * local + l],
                device_id=peer(to_line, place), device_id_type=MESH)

        @pl.when(line < outer - 1)
        def _():
            own_copy(line + 1, w_up).start()

        @pl.when(line > 0)
        def _():
            own_copy(line - 1, w_down).start()

    send_own(0)

    def v_copy(j, to, frm):
        return pltpu.make_async_remote_copy(
            src_ref=pack_v.at[to, j], dst_ref=vbuf.at[core, j, frm],
            send_sem=v_send.at[to * slots + j], recv_sem=v_recv.at[frm * slots + j],
            device_id=peer(line, to), device_id_type=MESH)

    def c_copy(j, to, frm):
        return pltpu.make_async_remote_copy(
            src_ref=pack_c.at[to, j], dst_ref=cbuf.at[j, frm],
            send_sem=c_send.at[to * slots + j], recv_sem=c_recv.at[frm * slots + j],
            device_id=peer(line, to), device_id_type=MESH)

    def fill(dst, src, first):
        for i in range(cap):
            dst[i * bands:(i + 1) * bands, :] = src[source_row[first + i]]

    relay = inner == 4
    across_x = place + 1 - 2 * lax.rem(place, 2)
    across_y = place + 2 - 4 * (place // 2)
    diagonal = inner - 1 - place

    def v_first(j):
        return pltpu.make_async_remote_copy(
            src_ref=pack_v.at[diagonal, j], dst_ref=hop_v.at[j],
            send_sem=v_send.at[diagonal * slots + j], recv_sem=hop_recv.at[j],
            device_id=peer(line, across_x), device_id_type=MESH)

    def c_first(j):
        return pltpu.make_async_remote_copy(
            src_ref=pack_c.at[diagonal, j], dst_ref=hop_c.at[j],
            send_sem=c_send.at[diagonal * slots + j], recv_sem=hop_recv.at[slots + j],
            device_id=peer(line, across_y), device_id_type=MESH)

    def v_second(j):
        return pltpu.make_async_remote_copy(
            src_ref=hop_v.at[j], dst_ref=vbuf.at[core, j, across_x],
            send_sem=hop_send.at[j], recv_sem=v_recv.at[across_x * slots + j],
            device_id=peer(line, across_y), device_id_type=MESH)

    def c_second(j):
        return pltpu.make_async_remote_copy(
            src_ref=hop_c.at[j], dst_ref=cbuf.at[j, across_y],
            send_sem=hop_send.at[slots + j], recv_sem=c_recv.at[across_y * slots + j],
            device_id=peer(line, across_x), device_id_type=MESH)

    def hand_on(j):
        v_first(j).wait_recv()
        v_second(j).start()
        c_first(j).wait_recv()
        c_second(j).start()

    def pack_val(j):
        if relay:
            fill(pack_v.at[diagonal, j], val_in, (diagonal * slots + j) * cap)
            v_first(j).start()
            for to in (across_x, across_y):
                fill(pack_v.at[to, j], val_in, (to * slots + j) * cap)
                v_copy(j, to, place).start()
            fill(vbuf.at[core, j, place], val_in, (place * slots + j) * cap)
            return

        def pack_to(d, carry):
            to = lax.rem(place + d, inner)
            fill(pack_v.at[to, j], val_in, (to * slots + j) * cap)
            v_copy(j, to, place).start()
            return carry

        lax.fori_loop(1, inner, pack_to, 0)
        fill(vbuf.at[core, j, place], val_in, (place * slots + j) * cap)

    def pack_cond(j):
        if relay:
            fill(pack_c.at[diagonal, j], cond_in, (diagonal * slots + j) * cap)
            c_first(j).start()
            for to in (across_x, across_y):
                fill(pack_c.at[to, j], cond_in, (to * slots + j) * cap)
                c_copy(j, to, place).start()
            fill(cbuf.at[j, place], cond_in, (place * slots + j) * cap)
            return

        def pack_to(d, carry):
            to = lax.rem(place + d, inner)
            fill(pack_c.at[to, j], cond_in, (to * slots + j) * cap)
            c_copy(j, to, place).start()
            return carry

        lax.fori_loop(1, inner, pack_to, 0)
        fill(cbuf.at[j, place], cond_in, (place * slots + j) * cap)

    def pack_step(step, carry):
        j = slot_at(step)
        pack_val(j)
        pack_cond(j)
        return carry

    copy_val.wait()
    copy_cond.start()
    copy_w.start()
    pack_val(slot_at(0))
    copy_cond.wait()
    pack_cond(slot_at(0))
    lax.fori_loop(1, WINDOW, pack_step, 0)
    copy_w.wait()

    def w_event(t, l):
        below, above = line - t, line + t

        @pl.when(below >= 0)
        def _():
            w_copy(below * local + l, line, w_up).wait_recv()

            @pl.when(line < outer - 1)
            def _():
                w_copy(below * local + l, line + 1, w_up).start()

        @pl.when(above < outer)
        def _():
            w_copy(above * local + l, line, w_down).wait_recv()

            @pl.when(line > 0)
            def _():
                w_copy(above * local + l, line - 1, w_down).start()

    def s_copy(j):
        return pltpu.make_async_remote_copy(
            src_ref=vbuf.at[core, j], dst_ref=vbuf.at[core, j], send_sem=s_send.at[j],
            recv_sem=s_recv.at[j], device_id=sibling, device_id_type=MESH)

    def s_arrived(j):
        return pltpu.make_async_remote_copy(
            src_ref=vbuf.at[1 - core, j], dst_ref=vbuf.at[1 - core, j], send_sem=s_send.at[j],
            recv_sem=s_recv.at[j], device_id=sibling, device_id_type=MESH)

    nt = (((1,), (1,)), ((), ()))
    width = app.shape[1]
    g_all = app.shape[2]
    g_tile = min(256, g_all)
    row_pair = lax.broadcasted_iota(jnp.int32, (rows, width), 0) // bands
    col_pair = lax.broadcasted_iota(jnp.int32, (rows, width), 1) // bands
    same_pair = row_pair == col_pair
    own_lane = (lax.broadcasted_iota(jnp.int32, (cap, bands // 2, 128), 1)
                == lax.broadcasted_iota(jnp.int32, (cap, bands // 2, 128), 2) // bands)

    def compute(j):
        def apply_tile(gt, carry):
            cols = pl.ds(pl.multiple_of(gt * g_tile, g_tile), g_tile)
            total = jnp.zeros((inner * rows, g_tile), jnp.float32)
            for h in range(2):
                total = total + lax.dot_general(
                    vbuf[h, j].reshape(inner * rows, half),
                    wbuf[j, cols, h * half:(h + 1) * half], nt,
                    preferred_element_type=jnp.float32)
            app[:, 0:rows, cols] = total.astype(jnp.bfloat16).reshape(inner, rows, g_tile)
            return carry

        lax.fori_loop(0, g_all // g_tile, apply_tile, 0)

        def take(d, carry):
            frm = lax.rem(place + d, inner)
            c_copy(j, frm, frm).wait_recv()
            return carry

        lax.fori_loop(1, inner, take, 0)

        def contract(s, carry):
            prod = lax.dot_general(cbuf[j, s], app[s], nt, preferred_element_type=jnp.float32)
            prod = jnp.where(same_pair, prod, 0.0)
            folded = prod[:, 0:128]
            for x in range(1, width // 128):
                folded = folded + prod[:, x * 128:(x + 1) * 128]
            shift = 64
            while shift >= bands:
                folded = folded + pltpu.roll(folded, shift, 1)
                shift //= 2
            folded = folded.reshape(cap, bands, 128)
            for h in range(2):
                piece = folded[:, h * (bands // 2):(h + 1) * (bands // 2), :]
                piece = jnp.sum(jnp.where(own_lane, piece, 0.0), axis=1)
                if cap_pad > cap:
                    piece = jnp.concatenate(
                        [piece, jnp.zeros((cap_pad - cap, 128), jnp.float32)], axis=0)
                part[h, j, s] = piece
            return carry

        lax.fori_loop(0, inner, contract, 0)

    events = {}
    count = (outer - 1) * local
    for e in range(count):
        events[1 + e * (slots + 1) // count] = (1 + e // local, e % local)

    def p_copy(j):
        return pltpu.make_async_remote_copy(
            src_ref=part.at[1 - core, j], dst_ref=sib.at[j], send_sem=p_send.at[j],
            recv_sem=p_recv.at[j], device_id=sibling, device_id_type=MESH)

    def r_copy(j, to, frm):
        return pltpu.make_async_remote_copy(
            src_ref=back.at[to, j], dst_ref=ret.at[frm, j], send_sem=r_send.at[to * slots + j],
            recv_sem=r_recv.at[frm * slots + j], device_id=peer(line, to), device_id_type=MESH)

    def work(step, carry):
        if relay:
            @pl.when(step + 1 < slots)
            def _():
                hand_on(slot_at(step + 1))

        @pl.when(step < slots)
        def _():
            j = slot_at(step)

            def take(d, carry):
                frm = lax.rem(place + d, inner)
                v_copy(j, frm, frm).wait_recv()
                return carry

            lax.fori_loop(1, inner, take, 0)
            s_copy(j).start()

        for l in range(1, local):
            @pl.when(step == l - 1)
            def _():
                send_own(l)

        @pl.when(step + WINDOW < slots)
        def _():
            pack_step(step + WINDOW, 0)

        for k, (t, l) in events.items():
            @pl.when(step == k)
            def _():
                w_event(t, l)

        @pl.when(step > 1)
        def _():
            j = slot_at(step - 2)
            p_copy(j).wait_recv()

            def give(d, carry):
                to = lax.rem(place + d, inner)
                back[to, j] = part[core, j, to] + sib[j, to]
                r_copy(j, to, place).start()
                return carry

            lax.fori_loop(1, inner, give, 0)
            ret[place, j] = part[core, j, place] + sib[j, place]

        @pl.when((step > 0) & (step <= slots))
        def _():
            j = slot_at(step - 1)
            s_arrived(j).wait_recv()

            compute(j)
            p_copy(j).start()

        return carry

    if relay:
        hand_on(slot_at(0))
    lax.fori_loop(0, slots + 2, work, 0)

    def settle(j, carry):
        def sent(d, carry):
            to = lax.rem(place + d, inner)
            v_copy(j, to, place).wait_send()
            c_copy(j, to, place).wait_send()
            return carry

        lax.fori_loop(1, inner, sent, 0)
        if relay:
            v_second(j).wait_send()
            c_second(j).wait_send()
        s_copy(j).wait_send()
        p_copy(j).wait_send()

        @pl.when((line < outer - 1) & (j // local <= line))
        def _():
            w_copy(j, line + 1, w_up).wait_send()

        @pl.when((line > 0) & (j // local >= line))
        def _():
            w_copy(j, line - 1, w_down).wait_send()

        return carry

    lax.fori_loop(0, slots, settle, 0)

    def got(j, carry):
        def each(d, carry):
            other = lax.rem(place + d, inner)
            r_copy(j, other, other).wait_recv()
            r_copy(j, other, place).wait_send()
            return carry

        return lax.fori_loop(1, inner, each, carry)

    lax.fori_loop(0, slots, got, 0)

    flat = ret.reshape(inner * slots * cap_pad, 128)

    def place_rows(b, carry):
        for i in range(8):
            row = b * 8 + i
            out_ref[pl.ds(row, 1), :] = flat[pl.ds(target[row], 1), :]
        return carry

    lax.fori_loop(0, out_ref.shape[0] // 8, place_rows, 0)


def visit_order(outer, local):
    steps = []
    for z in range(outer):
        order = [z * local + l for l in range(local)]
        for t in range(1, outer):
            for l in range(local):
                order += [y * local + l for y in (z - t, z + t) if 0 <= y < outer]
        steps.append(order)
    return steps


def body(peer_count, q_of_pair, q_slot, valence, conduction, screened):
    pair_count, bands, half = valence.shape
    local, g_rows, g_cols = screened.shape
    q_total = q_slot.shape[0]
    cap = max(2, (3 * pair_count + 2 * q_total - 1) // (2 * q_total))
    cap_pad = -(-cap // 8) * 8
    outer = 4 if peer_count % 4 == 0 else 1
    inner = peer_count // outer
    slots = outer * local
    rows = cap * bands
    width = -(-rows // 128) * 128

    q_ids = q_of_pair[:, 0]
    q_match = q_ids[:, None] == jnp.arange(q_total, dtype=jnp.int32)[None, :]
    slot_index = jnp.sum(jnp.where(q_match, q_slot[None, :], 0), axis=1)
    order_row = jnp.arange(pair_count, dtype=jnp.int32)
    same_q = (q_ids[:, None] == q_ids[None, :]) & (order_row[None, :] < order_row[:, None])
    rank = jnp.sum(same_q.astype(jnp.int32), axis=1)
    owner = slot_index // local
    group = owner % inner * slots + owner // inner * local + slot_index % local
    packed = group * cap + rank
    target = group * cap_pad + rank
    hit = packed[None, :] == jnp.arange(inner * slots * cap, dtype=jnp.int32)[:, None]
    source_row = jnp.sum(jnp.where(hit, order_row[None, :], 0), axis=1)

    smem = pl.BlockSpec(memory_space=pltpu.SMEM)
    anywhere = pl.BlockSpec(memory_space=pl.ANY)
    dma = pltpu.SemaphoreType.DMA
    bf16, f32 = jnp.bfloat16, jnp.float32
    return pl.pallas_call(
        functools.partial(kernel, outer, inner, local, cap, cap_pad, visit_order(outer, local)),
        out_shape=jax.ShapeDtypeStruct((pair_count, bands * bands // 2), f32),
        in_specs=[smem, smem, anywhere, anywhere, anywhere],
        out_specs=pl.BlockSpec(memory_space=pltpu.VMEM),
        scratch_shapes=[
            pltpu.VMEM((pair_count, bands, half), bf16),
            pltpu.VMEM((pair_count, bands, half), bf16),
            pltpu.VMEM((inner, slots, rows, half), bf16),
            pltpu.VMEM((inner, slots, rows, half), bf16),
            pltpu.VMEM((2, slots, inner, rows, half), bf16),
            pltpu.VMEM((slots, inner, rows, half), bf16),
            pltpu.VMEM((slots, g_rows, g_cols), bf16),
            pltpu.VMEM((slots, rows, half), bf16),
            pltpu.VMEM((slots, rows, half), bf16),
            pltpu.VMEM((inner, width, g_rows), bf16),
            pltpu.VMEM((2, slots, inner, cap_pad, 128), f32),
            pltpu.VMEM((slots, inner, cap_pad, 128), f32),
            pltpu.VMEM((inner, slots, cap_pad, 128), f32),
            pltpu.VMEM((inner, slots, cap_pad, 128), f32),
            dma((3,)), dma((slots,)), dma((slots,)), dma((slots,)),
            dma((inner * slots,)), dma((inner * slots,)),
            dma((inner * slots,)), dma((inner * slots,)),
            dma((slots,)), dma((slots,)), dma((slots,)), dma((slots,)),
            dma((inner * slots,)), dma((inner * slots,)),
            dma((2 * slots,)), dma((2 * slots,)),
        ],
        compiler_params=pltpu.CompilerParams(
            collective_id=0, has_side_effects=True, vmem_limit_bytes=58 * 1024 * 1024),
        cost_estimate=pl.CostEstimate(
            flops=2 * inner * slots * rows * g_rows * g_cols, transcendentals=0,
            bytes_accessed=4 * pair_count * bands * half + 2 * local * g_rows * g_cols),
    )(source_row, target, valence, conduction, screened)


def solution(mesh):
    in_specs = (P("pb", None), P(), P("pb", None, "ga"), P("pb", None, "ga"), P("pb", "ga", None))
    return jax.shard_map(functools.partial(body, mesh.shape["pb"]), mesh=mesh, in_specs=in_specs,
                         out_specs=P("pb", "ga"), check_vma=False)
```

```python
import functools

import jax
import jax.numpy as jnp
from jax import lax
from jax.experimental import pallas as pl
from jax.experimental.pallas import tpu as pltpu
from jax.sharding import PartitionSpec as P

MESH = pl.DeviceIdType.MESH
WINDOW = 3


def kernel(outer, inner, local, cap, cap_pad, steps,
           source_row, target, val_hbm, cond_hbm, w_hbm, out_ref,
           val_in, cond_in, pack_v, pack_c, vbuf, cbuf, wbuf, app, part, sib, back, ret,
           in_sem, w_up, w_down, w_recv, v_send, c_send, v_recv, c_recv,
           s_send, s_recv, p_send, p_recv, r_send, r_recv):
    me = lax.axis_index("pb")
    core = lax.axis_index("ga")
    line, place = me // inner, lax.rem(me, inner)
    bands = val_in.shape[1]
    rows = cap * bands
    slots = outer * local
    half = val_in.shape[2]

    def peer(to_line, to_place):
        return (to_line * inner + to_place, core)

    sibling = (me, 1 - core)

    def slot_at(step):
        found = jnp.int32(0)
        for z in range(outer):
            for k, j in enumerate(steps[z]):
                found = jnp.where((line == z) & (step == k), jnp.int32(j), found)
        return found

    barrier = pltpu.get_barrier_semaphore()
    pl.semaphore_signal(barrier, inc=1, device_id=sibling, device_id_type=MESH)
    for d in range(1, inner):
        pl.semaphore_signal(barrier, inc=1, device_id=peer(line, lax.rem(place + d, inner)),
                            device_id_type=MESH)

    @pl.when(line > 0)
    def _():
        pl.semaphore_signal(barrier, inc=1, device_id=peer(line - 1, place), device_id_type=MESH)

    @pl.when(line < outer - 1)
    def _():
        pl.semaphore_signal(barrier, inc=1, device_id=peer(line + 1, place), device_id_type=MESH)

    copy_val = pltpu.make_async_copy(val_hbm, val_in, in_sem.at[0])
    copy_cond = pltpu.make_async_copy(cond_hbm, cond_in, in_sem.at[1])
    copy_w = pltpu.make_async_copy(w_hbm, wbuf.at[pl.ds(line * local, local)], in_sem.at[2])
    copy_val.start()
    app[...] = jnp.zeros_like(app)
    pl.semaphore_wait(barrier, inner + (line > 0).astype(jnp.int32)
                      + (line < outer - 1).astype(jnp.int32))

    def w_copy(j, to_line, send):
        return pltpu.make_async_remote_copy(
            src_ref=wbuf.at[j], dst_ref=wbuf.at[j], send_sem=send.at[j],
            recv_sem=w_recv.at[j], device_id=peer(to_line, place), device_id_type=MESH)

    def send_own(l):
        def own_copy(to_line, send):
            return pltpu.make_async_remote_copy(
                src_ref=w_hbm.at[l], dst_ref=wbuf.at[line * local + l],
                send_sem=send.at[line * local + l], recv_sem=w_recv.at[line * local + l],
                device_id=peer(to_line, place), device_id_type=MESH)

        @pl.when(line < outer - 1)
        def _():
            own_copy(line + 1, w_up).start()

        @pl.when(line > 0)
        def _():
            own_copy(line - 1, w_down).start()

    for l in range(local):
        send_own(l)

    def v_copy(j, to, frm):
        return pltpu.make_async_remote_copy(
            src_ref=pack_v.at[to, j], dst_ref=vbuf.at[core, j, frm],
            send_sem=v_send.at[to * slots + j], recv_sem=v_recv.at[frm * slots + j],
            device_id=peer(line, to), device_id_type=MESH)

    def c_copy(j, to, frm):
        return pltpu.make_async_remote_copy(
            src_ref=pack_c.at[to, j], dst_ref=cbuf.at[j, frm],
            send_sem=c_send.at[to * slots + j], recv_sem=c_recv.at[frm * slots + j],
            device_id=peer(line, to), device_id_type=MESH)

    def fill(dst, src, first):
        for i in range(cap):
            dst[i * bands:(i + 1) * bands, :] = src[source_row[first + i]]

    def pack_val(j):
        def pack_to(d, carry):
            to = lax.rem(place + d, inner)
            fill(pack_v.at[to, j], val_in, (to * slots + j) * cap)
            v_copy(j, to, place).start()
            return carry

        lax.fori_loop(1, inner, pack_to, 0)
        fill(vbuf.at[core, j, place], val_in, (place * slots + j) * cap)

    def pack_cond(j):
        def pack_to(d, carry):
            to = lax.rem(place + d, inner)
            fill(pack_c.at[to, j], cond_in, (to * slots + j) * cap)
            c_copy(j, to, place).start()
            return carry

        lax.fori_loop(1, inner, pack_to, 0)
        fill(cbuf.at[j, place], cond_in, (place * slots + j) * cap)

    def pack_step(step, carry):
        j = slot_at(step)
        pack_val(j)
        pack_cond(j)
        return carry

    copy_val.wait()
    copy_cond.start()
    copy_w.start()
    pack_val(slot_at(0))
    copy_cond.wait()
    pack_cond(slot_at(0))
    lax.fori_loop(1, WINDOW, pack_step, 0)
    copy_w.wait()

    def w_event(t, l):
        below, above = line - t, line + t

        @pl.when(below >= 0)
        def _():
            w_copy(below * local + l, line, w_up).wait_recv()

            @pl.when(line < outer - 1)
            def _():
                w_copy(below * local + l, line + 1, w_up).start()

        @pl.when(above < outer)
        def _():
            w_copy(above * local + l, line, w_down).wait_recv()

            @pl.when(line > 0)
            def _():
                w_copy(above * local + l, line - 1, w_down).start()

    def s_copy(j):
        return pltpu.make_async_remote_copy(
            src_ref=vbuf.at[core, j], dst_ref=vbuf.at[core, j], send_sem=s_send.at[j],
            recv_sem=s_recv.at[j], device_id=sibling, device_id_type=MESH)

    def s_arrived(j):
        return pltpu.make_async_remote_copy(
            src_ref=vbuf.at[1 - core, j], dst_ref=vbuf.at[1 - core, j], send_sem=s_send.at[j],
            recv_sem=s_recv.at[j], device_id=sibling, device_id_type=MESH)

    nt = (((1,), (1,)), ((), ()))
    width = app.shape[1]
    g_all = app.shape[2]
    g_tile = min(256, g_all)
    row_pair = lax.broadcasted_iota(jnp.int32, (rows, width), 0) // bands
    col_pair = lax.broadcasted_iota(jnp.int32, (rows, width), 1) // bands
    same_pair = row_pair == col_pair
    own_lane = (lax.broadcasted_iota(jnp.int32, (cap, bands // 2, 128), 1)
                == lax.broadcasted_iota(jnp.int32, (cap, bands // 2, 128), 2) // bands)

    def compute(j):
        def apply_tile(gt, carry):
            cols = pl.ds(pl.multiple_of(gt * g_tile, g_tile), g_tile)
            total = jnp.zeros((inner * rows, g_tile), jnp.float32)
            for h in range(2):
                total = total + lax.dot_general(
                    vbuf[h, j].reshape(inner * rows, half),
                    wbuf[j, cols, h * half:(h + 1) * half], nt,
                    preferred_element_type=jnp.float32)
            app[:, 0:rows, cols] = total.astype(jnp.bfloat16).reshape(inner, rows, g_tile)
            return carry

        lax.fori_loop(0, g_all // g_tile, apply_tile, 0)

        def contract(d, carry):
            s = lax.rem(place + d, inner)

            @pl.when(d > 0)
            def _():
                c_copy(j, s, s).wait_recv()

            prod = lax.dot_general(cbuf[j, s], app[s], nt, preferred_element_type=jnp.float32)
            prod = jnp.where(same_pair, prod, 0.0)
            folded = prod[:, 0:128]
            for x in range(1, width // 128):
                folded = folded + prod[:, x * 128:(x + 1) * 128]
            shift = 64
            while shift >= bands:
                folded = folded + pltpu.roll(folded, shift, 1)
                shift //= 2
            folded = folded.reshape(cap, bands, 128)
            for h in range(2):
                piece = folded[:, h * (bands // 2):(h + 1) * (bands // 2), :]
                piece = jnp.sum(jnp.where(own_lane, piece, 0.0), axis=1)
                if cap_pad > cap:
                    piece = jnp.concatenate(
                        [piece, jnp.zeros((cap_pad - cap, 128), jnp.float32)], axis=0)
                part[h, j, s] = piece
            return carry

        lax.fori_loop(0, inner, contract, 0)

    events = {}
    count = (outer - 1) * local
    for e in range(count):
        events[1 + e * (slots + 1) // count] = (1 + e // local, e % local)

    def p_copy(j):
        return pltpu.make_async_remote_copy(
            src_ref=part.at[1 - core, j], dst_ref=sib.at[j], send_sem=p_send.at[j],
            recv_sem=p_recv.at[j], device_id=sibling, device_id_type=MESH)

    def r_copy(j, to, frm):
        return pltpu.make_async_remote_copy(
            src_ref=back.at[to, j], dst_ref=ret.at[frm, j], send_sem=r_send.at[to * slots + j],
            recv_sem=r_recv.at[frm * slots + j], device_id=peer(line, to), device_id_type=MESH)

    def work(step, carry):
        for k, (t, l) in events.items():
            if t < outer - 1:
                @pl.when(step == k)
                def _():
                    w_event(t, l)

        @pl.when(step < slots)
        def _():
            j = slot_at(step)

            def take(d, carry):
                frm = lax.rem(place + d, inner)
                v_copy(j, frm, frm).wait_recv()
                return carry

            lax.fori_loop(1, inner, take, 0)
            s_copy(j).start()

        @pl.when(step + WINDOW < slots)
        def _():
            pack_step(step + WINDOW, 0)

        for k, (t, l) in events.items():
            if t == outer - 1:
                @pl.when(step == k)
                def _():
                    w_event(t, l)

        @pl.when(step > 1)
        def _():
            j = slot_at(step - 2)
            p_copy(j).wait_recv()

            def give(d, carry):
                to = lax.rem(place + d, inner)
                back[to, j] = part[core, j, to] + sib[j, to]
                r_copy(j, to, place).start()
                return carry

            lax.fori_loop(1, inner, give, 0)
            ret[place, j] = part[core, j, place] + sib[j, place]

        @pl.when((step > 0) & (step <= slots))
        def _():
            j = slot_at(step - 1)
            s_arrived(j).wait_recv()

            compute(j)
            p_copy(j).start()

        return carry

    lax.fori_loop(0, slots + 2, work, 0)

    def settle(j, carry):
        def sent(d, carry):
            to = lax.rem(place + d, inner)
            v_copy(j, to, place).wait_send()
            c_copy(j, to, place).wait_send()
            return carry

        lax.fori_loop(1, inner, sent, 0)
        s_copy(j).wait_send()
        p_copy(j).wait_send()

        @pl.when((line < outer - 1) & (j // local <= line))
        def _():
            w_copy(j, line + 1, w_up).wait_send()

        @pl.when((line > 0) & (j // local >= line))
        def _():
            w_copy(j, line - 1, w_down).wait_send()

        return carry

    lax.fori_loop(0, slots, settle, 0)

    def got(j, carry):
        def each(d, carry):
            other = lax.rem(place + d, inner)
            r_copy(j, other, other).wait_recv()
            r_copy(j, other, place).wait_send()
            return carry

        return lax.fori_loop(1, inner, each, carry)

    lax.fori_loop(0, slots, got, 0)

    flat = ret.reshape(inner * slots * cap_pad, 128)

    def place_rows(b, carry):
        for i in range(8):
            row = b * 8 + i
            out_ref[pl.ds(row, 1), :] = flat[pl.ds(target[row], 1), :]
        return carry

    lax.fori_loop(0, out_ref.shape[0] // 8, place_rows, 0)


def visit_order(outer, local):
    steps = []
    for z in range(outer):
        order = [z * local + l for l in range(local)]
        for t in range(1, outer):
            for l in range(local):
                order += [y * local + l for y in (z - t, z + t) if 0 <= y < outer]
        steps.append(order)
    return steps


def body(peer_count, q_of_pair, q_slot, valence, conduction, screened):
    pair_count, bands, half = valence.shape
    local, g_rows, g_cols = screened.shape
    q_total = q_slot.shape[0]
    cap = max(2, (3 * pair_count + 2 * q_total - 1) // (2 * q_total))
    cap_pad = -(-cap // 8) * 8
    outer = 4 if peer_count % 4 == 0 else 1
    inner = peer_count // outer
    slots = outer * local
    rows = cap * bands
    width = -(-rows // 128) * 128

    q_ids = q_of_pair[:, 0]
    q_match = q_ids[:, None] == jnp.arange(q_total, dtype=jnp.int32)[None, :]
    slot_index = jnp.sum(jnp.where(q_match, q_slot[None, :], 0), axis=1)
    order_row = jnp.arange(pair_count, dtype=jnp.int32)
    same_q = (q_ids[:, None] == q_ids[None, :]) & (order_row[None, :] < order_row[:, None])
    rank = jnp.sum(same_q.astype(jnp.int32), axis=1)
    owner = slot_index // local
    group = owner % inner * slots + owner // inner * local + slot_index % local
    packed = group * cap + rank
    target = group * cap_pad + rank
    hit = packed[None, :] == jnp.arange(inner * slots * cap, dtype=jnp.int32)[:, None]
    source_row = jnp.sum(jnp.where(hit, order_row[None, :], 0), axis=1)

    smem = pl.BlockSpec(memory_space=pltpu.SMEM)
    anywhere = pl.BlockSpec(memory_space=pl.ANY)
    dma = pltpu.SemaphoreType.DMA
    bf16, f32 = jnp.bfloat16, jnp.float32
    return pl.pallas_call(
        functools.partial(kernel, outer, inner, local, cap, cap_pad, visit_order(outer, local)),
        out_shape=jax.ShapeDtypeStruct((pair_count, bands * bands // 2), f32),
        in_specs=[smem, smem, anywhere, anywhere, anywhere],
        out_specs=pl.BlockSpec(memory_space=pltpu.VMEM),
        scratch_shapes=[
            pltpu.VMEM((pair_count, bands, half), bf16),
            pltpu.VMEM((pair_count, bands, half), bf16),
            pltpu.VMEM((inner, slots, rows, half), bf16),
            pltpu.VMEM((inner, slots, rows, half), bf16),
            pltpu.VMEM((2, slots, inner, rows, half), bf16),
            pltpu.VMEM((slots, inner, rows, half), bf16),
            pltpu.VMEM((slots, g_rows, g_cols), bf16),
            pltpu.VMEM((inner, width, g_rows), bf16),
            pltpu.VMEM((2, slots, inner, cap_pad, 128), f32),
            pltpu.VMEM((slots, inner, cap_pad, 128), f32),
            pltpu.VMEM((inner, slots, cap_pad, 128), f32),
            pltpu.VMEM((inner, slots, cap_pad, 128), f32),
            dma((3,)), dma((slots,)), dma((slots,)), dma((slots,)),
            dma((inner * slots,)), dma((inner * slots,)),
            dma((inner * slots,)), dma((inner * slots,)),
            dma((slots,)), dma((slots,)), dma((slots,)), dma((slots,)),
            dma((inner * slots,)), dma((inner * slots,)),
        ],
        compiler_params=pltpu.CompilerParams(
            collective_id=0, has_side_effects=True, vmem_limit_bytes=58 * 1024 * 1024),
        cost_estimate=pl.CostEstimate(
            flops=2 * inner * slots * rows * g_rows * g_cols, transcendentals=0,
            bytes_accessed=4 * pair_count * bands * half + 2 * local * g_rows * g_cols),
    )(source_row, target, valence, conduction, screened)


def solution(mesh):
    in_specs = (P("pb", None), P(), P("pb", None, "ga"), P("pb", None, "ga"), P("pb", "ga", None))
    return jax.shard_map(functools.partial(body, mesh.shape["pb"]), mesh=mesh, in_specs=in_specs,
                         out_specs=P("pb", "ga"), check_vma=False)
```

```python
import functools

import jax
import jax.numpy as jnp
from jax import lax
from jax.experimental import pallas as pl
from jax.experimental.pallas import tpu as pltpu
from jax.sharding import PartitionSpec as P

MESH = pl.DeviceIdType.MESH
WINDOW = 3


def kernel(outer, inner, local, cap, cap_pad, steps,
           source_row, target, val_hbm, cond_hbm, w_hbm, out_ref,
           val_in, cond_in, pack_v, pack_c, vbuf, cbuf, wbuf, app, part, sib, back, ret,
           in_sem, w_up, w_down, w_recv, v_send, c_send, v_recv, c_recv,
           s_send, s_recv, p_send, p_recv, r_send, r_recv):
    me = lax.axis_index("pb")
    core = lax.axis_index("ga")
    line, place = me // inner, lax.rem(me, inner)
    bands = val_in.shape[1]
    rows = cap * bands
    slots = outer * local
    half = val_in.shape[2]

    def peer(to_line, to_place):
        return (to_line * inner + to_place, core)

    sibling = (me, 1 - core)

    def slot_at(step):
        found = jnp.int32(0)
        for z in range(outer):
            for k, j in enumerate(steps[z]):
                found = jnp.where((line == z) & (step == k), jnp.int32(j), found)
        return found

    barrier = pltpu.get_barrier_semaphore()
    pl.semaphore_signal(barrier, inc=1, device_id=sibling, device_id_type=MESH)
    for d in range(1, inner):
        pl.semaphore_signal(barrier, inc=1, device_id=peer(line, lax.rem(place + d, inner)),
                            device_id_type=MESH)

    @pl.when(line > 0)
    def _():
        pl.semaphore_signal(barrier, inc=1, device_id=peer(line - 1, place), device_id_type=MESH)

    @pl.when(line < outer - 1)
    def _():
        pl.semaphore_signal(barrier, inc=1, device_id=peer(line + 1, place), device_id_type=MESH)

    copy_val = pltpu.make_async_copy(val_hbm, val_in, in_sem.at[0])
    copy_cond = pltpu.make_async_copy(cond_hbm, cond_in, in_sem.at[1])
    copy_w = pltpu.make_async_copy(w_hbm, wbuf.at[pl.ds(line * local, local)], in_sem.at[2])
    copy_val.start()
    app[...] = jnp.zeros_like(app)
    pl.semaphore_wait(barrier, inner + (line > 0).astype(jnp.int32)
                      + (line < outer - 1).astype(jnp.int32))

    def w_copy(j, to_line, send):
        return pltpu.make_async_remote_copy(
            src_ref=wbuf.at[j], dst_ref=wbuf.at[j], send_sem=send.at[j],
            recv_sem=w_recv.at[j], device_id=peer(to_line, place), device_id_type=MESH)

    def send_own(l):
        def own_copy(to_line, send):
            return pltpu.make_async_remote_copy(
                src_ref=w_hbm.at[l], dst_ref=wbuf.at[line * local + l],
                send_sem=send.at[line * local + l], recv_sem=w_recv.at[line * local + l],
                device_id=peer(to_line, place), device_id_type=MESH)

        @pl.when(line < outer - 1)
        def _():
            own_copy(line + 1, w_up).start()

        @pl.when(line > 0)
        def _():
            own_copy(line - 1, w_down).start()

    for l in range(local):
        send_own(l)

    def v_copy(j, to, frm):
        return pltpu.make_async_remote_copy(
            src_ref=pack_v.at[to, j], dst_ref=vbuf.at[core, j, frm],
            send_sem=v_send.at[to * slots + j], recv_sem=v_recv.at[frm * slots + j],
            device_id=peer(line, to), device_id_type=MESH)

    def c_copy(j, to, frm):
        return pltpu.make_async_remote_copy(
            src_ref=pack_c.at[to, j], dst_ref=cbuf.at[j, frm],
            send_sem=c_send.at[to * slots + j], recv_sem=c_recv.at[frm * slots + j],
            device_id=peer(line, to), device_id_type=MESH)

    def fill(dst, src, first):
        for i in range(cap):
            dst[i * bands:(i + 1) * bands, :] = src[source_row[first + i]]

    def send_place(d):
        if inner != 4:
            return lax.rem(place + d, inner)
        across_x = place + 1 - 2 * lax.rem(place, 2)
        across_y = place + 2 - 4 * (place // 2)
        first = jnp.where(core == 0, across_x, across_y)
        second = jnp.where(core == 0, across_y, across_x)
        return jnp.where(d == 1, first, jnp.where(d == 2, second, inner - 1 - place))

    def pack_val(j):
        def pack_to(d, carry):
            to = send_place(d)
            fill(pack_v.at[to, j], val_in, (to * slots + j) * cap)
            v_copy(j, to, place).start()
            return carry

        lax.fori_loop(1, inner, pack_to, 0)
        fill(vbuf.at[core, j, place], val_in, (place * slots + j) * cap)

    def pack_cond(j):
        def pack_to(d, carry):
            to = send_place(d)
            fill(pack_c.at[to, j], cond_in, (to * slots + j) * cap)
            c_copy(j, to, place).start()
            return carry

        lax.fori_loop(1, inner, pack_to, 0)
        fill(cbuf.at[j, place], cond_in, (place * slots + j) * cap)

    def pack_step(step, carry):
        j = slot_at(step)
        pack_val(j)
        pack_cond(j)
        return carry

    copy_val.wait()
    copy_cond.start()
    copy_w.start()
    pack_val(slot_at(0))
    copy_cond.wait()
    pack_cond(slot_at(0))
    lax.fori_loop(1, WINDOW, pack_step, 0)
    copy_w.wait()

    def w_event(t, l):
        below, above = line - t, line + t

        @pl.when(below >= 0)
        def _():
            w_copy(below * local + l, line, w_up).wait_recv()

            @pl.when(line < outer - 1)
            def _():
                w_copy(below * local + l, line + 1, w_up).start()

        @pl.when(above < outer)
        def _():
            w_copy(above * local + l, line, w_down).wait_recv()

            @pl.when(line > 0)
            def _():
                w_copy(above * local + l, line - 1, w_down).start()

    def s_copy(j):
        return pltpu.make_async_remote_copy(
            src_ref=vbuf.at[core, j], dst_ref=vbuf.at[core, j], send_sem=s_send.at[j],
            recv_sem=s_recv.at[j], device_id=sibling, device_id_type=MESH)

    def s_arrived(j):
        return pltpu.make_async_remote_copy(
            src_ref=vbuf.at[1 - core, j], dst_ref=vbuf.at[1 - core, j], send_sem=s_send.at[j],
            recv_sem=s_recv.at[j], device_id=sibling, device_id_type=MESH)

    nt = (((1,), (1,)), ((), ()))
    width = app.shape[1]
    g_all = app.shape[2]
    g_tile = min(256, g_all)
    row_pair = lax.broadcasted_iota(jnp.int32, (rows, width), 0) // bands
    col_pair = lax.broadcasted_iota(jnp.int32, (rows, width), 1) // bands
    same_pair = row_pair == col_pair
    own_lane = (lax.broadcasted_iota(jnp.int32, (cap, bands // 2, 128), 1)
                == lax.broadcasted_iota(jnp.int32, (cap, bands // 2, 128), 2) // bands)

    def compute(j):
        def apply_tile(gt, carry):
            cols = pl.ds(pl.multiple_of(gt * g_tile, g_tile), g_tile)
            total = jnp.zeros((inner * rows, g_tile), jnp.float32)
            for h in range(2):
                total = total + lax.dot_general(
                    vbuf[h, j].reshape(inner * rows, half),
                    wbuf[j, cols, h * half:(h + 1) * half], nt,
                    preferred_element_type=jnp.float32)
            app[:, 0:rows, cols] = total.astype(jnp.bfloat16).reshape(inner, rows, g_tile)
            return carry

        lax.fori_loop(0, g_all // g_tile, apply_tile, 0)

        def contract(d, carry):
            s = lax.rem(place + d, inner)

            @pl.when(d > 0)
            def _():
                c_copy(j, s, s).wait_recv()

            prod = lax.dot_general(cbuf[j, s], app[s], nt, preferred_element_type=jnp.float32)
            prod = jnp.where(same_pair, prod, 0.0)
            folded = prod[:, 0:128]
            for x in range(1, width // 128):
                folded = folded + prod[:, x * 128:(x + 1) * 128]
            shift = 64
            while shift >= bands:
                folded = folded + pltpu.roll(folded, shift, 1)
                shift //= 2
            folded = folded.reshape(cap, bands, 128)
            for h in range(2):
                piece = folded[:, h * (bands // 2):(h + 1) * (bands // 2), :]
                piece = jnp.sum(jnp.where(own_lane, piece, 0.0), axis=1)
                if cap_pad > cap:
                    piece = jnp.concatenate(
                        [piece, jnp.zeros((cap_pad - cap, 128), jnp.float32)], axis=0)
                part[h, j, s] = piece
            return carry

        lax.fori_loop(0, inner, contract, 0)

    events = {}
    count = (outer - 1) * local
    for e in range(count):
        events[1 + e * (slots + 1) // count] = (1 + e // local, e % local)

    def p_copy(j):
        return pltpu.make_async_remote_copy(
            src_ref=part.at[1 - core, j], dst_ref=sib.at[j], send_sem=p_send.at[j],
            recv_sem=p_recv.at[j], device_id=sibling, device_id_type=MESH)

    def r_copy(j, to, frm):
        return pltpu.make_async_remote_copy(
            src_ref=back.at[to, j], dst_ref=ret.at[frm, j], send_sem=r_send.at[to * slots + j],
            recv_sem=r_recv.at[frm * slots + j], device_id=peer(line, to), device_id_type=MESH)

    def work(step, carry):
        for k, (t, l) in events.items():
            if t < outer - 1:
                @pl.when(step == k)
                def _():
                    w_event(t, l)

        @pl.when(step < slots)
        def _():
            j = slot_at(step)

            def take(d, carry):
                frm = lax.rem(place + d, inner)
                v_copy(j, frm, frm).wait_recv()
                return carry

            lax.fori_loop(1, inner, take, 0)
            s_copy(j).start()

        @pl.when(step + WINDOW < slots)
        def _():
            pack_step(step + WINDOW, 0)

        for k, (t, l) in events.items():
            if t == outer - 1:
                @pl.when(step == k)
                def _():
                    w_event(t, l)

        @pl.when(step > 1)
        def _():
            j = slot_at(step - 2)
            p_copy(j).wait_recv()

            def give(d, carry):
                to = lax.rem(place + d, inner)
                back[to, j] = part[core, j, to] + sib[j, to]
                r_copy(j, to, place).start()
                return carry

            lax.fori_loop(1, inner, give, 0)
            ret[place, j] = part[core, j, place] + sib[j, place]

        @pl.when((step > 0) & (step <= slots))
        def _():
            j = slot_at(step - 1)
            s_arrived(j).wait_recv()

            compute(j)
            p_copy(j).start()

        return carry

    lax.fori_loop(0, slots + 2, work, 0)

    def settle(j, carry):
        def sent(d, carry):
            to = lax.rem(place + d, inner)
            v_copy(j, to, place).wait_send()
            c_copy(j, to, place).wait_send()
            return carry

        lax.fori_loop(1, inner, sent, 0)
        s_copy(j).wait_send()
        p_copy(j).wait_send()

        @pl.when((line < outer - 1) & (j // local <= line))
        def _():
            w_copy(j, line + 1, w_up).wait_send()

        @pl.when((line > 0) & (j // local >= line))
        def _():
            w_copy(j, line - 1, w_down).wait_send()

        return carry

    lax.fori_loop(0, slots, settle, 0)

    def got(j, carry):
        def each(d, carry):
            other = lax.rem(place + d, inner)
            r_copy(j, other, other).wait_recv()
            r_copy(j, other, place).wait_send()
            return carry

        return lax.fori_loop(1, inner, each, carry)

    lax.fori_loop(0, slots, got, 0)

    flat = ret.reshape(inner * slots * cap_pad, 128)

    def place_rows(b, carry):
        for i in range(8):
            row = b * 8 + i
            out_ref[pl.ds(row, 1), :] = flat[pl.ds(target[row], 1), :]
        return carry

    lax.fori_loop(0, out_ref.shape[0] // 8, place_rows, 0)


def visit_order(outer, local):
    steps = []
    for z in range(outer):
        order = [z * local + l for l in range(local)]
        for t in range(1, outer):
            for l in range(local):
                order += [y * local + l for y in (z - t, z + t) if 0 <= y < outer]
        steps.append(order)
    return steps


def body(peer_count, q_of_pair, q_slot, valence, conduction, screened):
    pair_count, bands, half = valence.shape
    local, g_rows, g_cols = screened.shape
    q_total = q_slot.shape[0]
    cap = max(2, (3 * pair_count + 2 * q_total - 1) // (2 * q_total))
    cap_pad = -(-cap // 8) * 8
    outer = 4 if peer_count % 4 == 0 else 1
    inner = peer_count // outer
    slots = outer * local
    rows = cap * bands
    width = -(-rows // 128) * 128

    q_ids = q_of_pair[:, 0]
    q_match = q_ids[:, None] == jnp.arange(q_total, dtype=jnp.int32)[None, :]
    slot_index = jnp.sum(jnp.where(q_match, q_slot[None, :], 0), axis=1)
    order_row = jnp.arange(pair_count, dtype=jnp.int32)
    same_q = (q_ids[:, None] == q_ids[None, :]) & (order_row[None, :] < order_row[:, None])
    rank = jnp.sum(same_q.astype(jnp.int32), axis=1)
    owner = slot_index // local
    group = owner % inner * slots + owner // inner * local + slot_index % local
    packed = group * cap + rank
    target = group * cap_pad + rank
    hit = packed[None, :] == jnp.arange(inner * slots * cap, dtype=jnp.int32)[:, None]
    source_row = jnp.sum(jnp.where(hit, order_row[None, :], 0), axis=1)

    smem = pl.BlockSpec(memory_space=pltpu.SMEM)
    anywhere = pl.BlockSpec(memory_space=pl.ANY)
    dma = pltpu.SemaphoreType.DMA
    bf16, f32 = jnp.bfloat16, jnp.float32
    return pl.pallas_call(
        functools.partial(kernel, outer, inner, local, cap, cap_pad, visit_order(outer, local)),
        out_shape=jax.ShapeDtypeStruct((pair_count, bands * bands // 2), f32),
        in_specs=[smem, smem, anywhere, anywhere, anywhere],
        out_specs=pl.BlockSpec(memory_space=pltpu.VMEM),
        scratch_shapes=[
            pltpu.VMEM((pair_count, bands, half), bf16),
            pltpu.VMEM((pair_count, bands, half), bf16),
            pltpu.VMEM((inner, slots, rows, half), bf16),
            pltpu.VMEM((inner, slots, rows, half), bf16),
            pltpu.VMEM((2, slots, inner, rows, half), bf16),
            pltpu.VMEM((slots, inner, rows, half), bf16),
            pltpu.VMEM((slots, g_rows, g_cols), bf16),
            pltpu.VMEM((inner, width, g_rows), bf16),
            pltpu.VMEM((2, slots, inner, cap_pad, 128), f32),
            pltpu.VMEM((slots, inner, cap_pad, 128), f32),
            pltpu.VMEM((inner, slots, cap_pad, 128), f32),
            pltpu.VMEM((inner, slots, cap_pad, 128), f32),
            dma((3,)), dma((slots,)), dma((slots,)), dma((slots,)),
            dma((inner * slots,)), dma((inner * slots,)),
            dma((inner * slots,)), dma((inner * slots,)),
            dma((slots,)), dma((slots,)), dma((slots,)), dma((slots,)),
            dma((inner * slots,)), dma((inner * slots,)),
        ],
        compiler_params=pltpu.CompilerParams(
            collective_id=0, has_side_effects=True, vmem_limit_bytes=58 * 1024 * 1024),
        cost_estimate=pl.CostEstimate(
            flops=2 * inner * slots * rows * g_rows * g_cols, transcendentals=0,
            bytes_accessed=4 * pair_count * bands * half + 2 * local * g_rows * g_cols),
    )(source_row, target, valence, conduction, screened)


def solution(mesh):
    in_specs = (P("pb", None), P(), P("pb", None, "ga"), P("pb", None, "ga"), P("pb", "ga", None))
    return jax.shard_map(functools.partial(body, mesh.shape["pb"]), mesh=mesh, in_specs=in_specs,
                         out_specs=P("pb", "ga"), check_vma=False)
```

```python
import functools

import jax
import jax.numpy as jnp
from jax import lax
from jax.experimental import pallas as pl
from jax.experimental.pallas import tpu as pltpu
from jax.sharding import PartitionSpec as P

MESH = pl.DeviceIdType.MESH
WINDOW = 2


def kernel(outer, inner, local, cap, cap_pad, steps,
           source_row, target, val_hbm, cond_hbm, w_hbm, out_ref,
           val_in, cond_in, pack_v, pack_c, vbuf, cbuf, wbuf, app, part, sib, back, ret,
           in_sem, w_up, w_down, w_recv, v_send, c_send, v_recv, c_recv,
           s_send, s_recv, p_send, p_recv, r_send, r_recv):
    me = lax.axis_index("pb")
    core = lax.axis_index("ga")
    line, place = me // inner, lax.rem(me, inner)
    bands = val_in.shape[1]
    rows = cap * bands
    slots = outer * local
    half = val_in.shape[2]

    def peer(to_line, to_place):
        return (to_line * inner + to_place, core)

    sibling = (me, 1 - core)

    def slot_at(step):
        found = jnp.int32(0)
        for z in range(outer):
            for k, j in enumerate(steps[z]):
                found = jnp.where((line == z) & (step == k), jnp.int32(j), found)
        return found

    barrier = pltpu.get_barrier_semaphore()
    pl.semaphore_signal(barrier, inc=1, device_id=sibling, device_id_type=MESH)
    for d in range(1, inner):
        pl.semaphore_signal(barrier, inc=1, device_id=peer(line, lax.rem(place + d, inner)),
                            device_id_type=MESH)

    @pl.when(line > 0)
    def _():
        pl.semaphore_signal(barrier, inc=1, device_id=peer(line - 1, place), device_id_type=MESH)

    @pl.when(line < outer - 1)
    def _():
        pl.semaphore_signal(barrier, inc=1, device_id=peer(line + 1, place), device_id_type=MESH)

    copy_val = pltpu.make_async_copy(val_hbm, val_in, in_sem.at[0])
    copy_cond = pltpu.make_async_copy(cond_hbm, cond_in, in_sem.at[1])
    copy_w = pltpu.make_async_copy(w_hbm, wbuf.at[pl.ds(line * local, local)], in_sem.at[2])
    copy_val.start()
    app[...] = jnp.zeros_like(app)
    pl.semaphore_wait(barrier, inner + (line > 0).astype(jnp.int32)
                      + (line < outer - 1).astype(jnp.int32))

    def w_copy(j, to_line, send):
        return pltpu.make_async_remote_copy(
            src_ref=wbuf.at[j], dst_ref=wbuf.at[j], send_sem=send.at[j],
            recv_sem=w_recv.at[j], device_id=peer(to_line, place), device_id_type=MESH)

    def send_own(l):
        def own_copy(to_line, send):
            return pltpu.make_async_remote_copy(
                src_ref=w_hbm.at[l], dst_ref=wbuf.at[line * local + l],
                send_sem=send.at[line * local + l], recv_sem=w_recv.at[line * local + l],
                device_id=peer(to_line, place), device_id_type=MESH)

        @pl.when(line < outer - 1)
        def _():
            own_copy(line + 1, w_up).start()

        @pl.when(line > 0)
        def _():
            own_copy(line - 1, w_down).start()

    for l in range(local):
        send_own(l)

    def v_copy(j, to, frm):
        return pltpu.make_async_remote_copy(
            src_ref=pack_v.at[to, j], dst_ref=vbuf.at[core, j, frm],
            send_sem=v_send.at[to * slots + j], recv_sem=v_recv.at[frm * slots + j],
            device_id=peer(line, to), device_id_type=MESH)

    def c_copy(j, to, frm):
        return pltpu.make_async_remote_copy(
            src_ref=pack_c.at[to, j], dst_ref=cbuf.at[j, frm],
            send_sem=c_send.at[to * slots + j], recv_sem=c_recv.at[frm * slots + j],
            device_id=peer(line, to), device_id_type=MESH)

    def fill(dst, src, first):
        for i in range(cap):
            dst[i * bands:(i + 1) * bands, :] = src[source_row[first + i]]

    def pack_val(j):
        def pack_to(d, carry):
            to = lax.rem(place + d, inner)
            fill(pack_v.at[to, j], val_in, (to * slots + j) * cap)
            v_copy(j, to, place).start()
            return carry

        lax.fori_loop(1, inner, pack_to, 0)
        fill(vbuf.at[core, j, place], val_in, (place * slots + j) * cap)

    def pack_cond(j):
        def pack_to(d, carry):
            to = lax.rem(place + d, inner)
            fill(pack_c.at[to, j], cond_in, (to * slots + j) * cap)
            c_copy(j, to, place).start()
            return carry

        lax.fori_loop(1, inner, pack_to, 0)
        fill(cbuf.at[j, place], cond_in, (place * slots + j) * cap)

    def pack_step(step, carry):
        j = slot_at(step)
        pack_val(j)
        pack_cond(j)
        return carry

    copy_val.wait()
    copy_cond.start()
    copy_w.start()
    pack_val(slot_at(0))
    copy_cond.wait()
    pack_cond(slot_at(0))
    lax.fori_loop(1, WINDOW, pack_step, 0)
    copy_w.wait()

    def w_event(t, l):
        below, above = line - t, line + t

        @pl.when(below >= 0)
        def _():
            w_copy(below * local + l, line, w_up).wait_recv()

            @pl.when(line < outer - 1)
            def _():
                w_copy(below * local + l, line + 1, w_up).start()

        @pl.when(above < outer)
        def _():
            w_copy(above * local + l, line, w_down).wait_recv()

            @pl.when(line > 0)
            def _():
                w_copy(above * local + l, line - 1, w_down).start()

    def s_copy(j):
        return pltpu.make_async_remote_copy(
            src_ref=vbuf.at[core, j], dst_ref=vbuf.at[core, j], send_sem=s_send.at[j],
            recv_sem=s_recv.at[j], device_id=sibling, device_id_type=MESH)

    def s_arrived(j):
        return pltpu.make_async_remote_copy(
            src_ref=vbuf.at[1 - core, j], dst_ref=vbuf.at[1 - core, j], send_sem=s_send.at[j],
            recv_sem=s_recv.at[j], device_id=sibling, device_id_type=MESH)

    nt = (((1,), (1,)), ((), ()))
    width = app.shape[1]
    g_all = app.shape[2]
    g_tile = min(256, g_all)
    row_pair = lax.broadcasted_iota(jnp.int32, (rows, width), 0) // bands
    col_pair = lax.broadcasted_iota(jnp.int32, (rows, width), 1) // bands
    same_pair = row_pair == col_pair
    own_lane = (lax.broadcasted_iota(jnp.int32, (cap, bands // 2, 128), 1)
                == lax.broadcasted_iota(jnp.int32, (cap, bands // 2, 128), 2) // bands)

    def compute(j):
        def apply_tile(gt, carry):
            cols = pl.ds(pl.multiple_of(gt * g_tile, g_tile), g_tile)
            total = jnp.zeros((inner * rows, g_tile), jnp.float32)
            for h in range(2):
                total = total + lax.dot_general(
                    vbuf[h, j].reshape(inner * rows, half),
                    wbuf[j, cols, h * half:(h + 1) * half], nt,
                    preferred_element_type=jnp.float32)
            app[:, 0:rows, cols] = total.astype(jnp.bfloat16).reshape(inner, rows, g_tile)
            return carry

        lax.fori_loop(0, g_all // g_tile, apply_tile, 0)

        def contract(d, carry):
            s = lax.rem(place + d, inner)

            @pl.when(d > 0)
            def _():
                c_copy(j, s, s).wait_recv()

            prod = lax.dot_general(cbuf[j, s], app[s], nt, preferred_element_type=jnp.float32)
            prod = jnp.where(same_pair, prod, 0.0)
            folded = prod[:, 0:128]
            for x in range(1, width // 128):
                folded = folded + prod[:, x * 128:(x + 1) * 128]
            shift = 64
            while shift >= bands:
                folded = folded + pltpu.roll(folded, shift, 1)
                shift //= 2
            folded = folded.reshape(cap, bands, 128)
            for h in range(2):
                piece = folded[:, h * (bands // 2):(h + 1) * (bands // 2), :]
                piece = jnp.sum(jnp.where(own_lane, piece, 0.0), axis=1)
                if cap_pad > cap:
                    piece = jnp.concatenate(
                        [piece, jnp.zeros((cap_pad - cap, 128), jnp.float32)], axis=0)
                part[h, j, s] = piece
            return carry

        lax.fori_loop(0, inner, contract, 0)

    events = {}
    count = (outer - 1) * local
    for e in range(count):
        events[1 + e * (slots + 1) // count] = (1 + e // local, e % local)

    def p_copy(j):
        return pltpu.make_async_remote_copy(
            src_ref=part.at[1 - core, j], dst_ref=sib.at[j], send_sem=p_send.at[j],
            recv_sem=p_recv.at[j], device_id=sibling, device_id_type=MESH)

    def r_copy(j, to, frm):
        return pltpu.make_async_remote_copy(
            src_ref=back.at[to, j], dst_ref=ret.at[frm, j], send_sem=r_send.at[to * slots + j],
            recv_sem=r_recv.at[frm * slots + j], device_id=peer(line, to), device_id_type=MESH)

    def work(step, carry):
        for k, (t, l) in events.items():
            if t < outer - 1:
                @pl.when(step == k)
                def _():
                    w_event(t, l)

        @pl.when(step < slots)
        def _():
            j = slot_at(step)

            def take(d, carry):
                frm = lax.rem(place + d, inner)
                v_copy(j, frm, frm).wait_recv()
                return carry

            lax.fori_loop(1, inner, take, 0)
            s_copy(j).start()

        @pl.when(step + WINDOW < slots)
        def _():
            pack_step(step + WINDOW, 0)

        for k, (t, l) in events.items():
            if t == outer - 1:
                @pl.when(step == k)
                def _():
                    w_event(t, l)

        @pl.when(step > 1)
        def _():
            j = slot_at(step - 2)
            p_copy(j).wait_recv()

            def give(d, carry):
                to = lax.rem(place + d, inner)
                back[to, j] = part[core, j, to] + sib[j, to]
                r_copy(j, to, place).start()
                return carry

            lax.fori_loop(1, inner, give, 0)
            ret[place, j] = part[core, j, place] + sib[j, place]

        @pl.when((step > 0) & (step <= slots))
        def _():
            j = slot_at(step - 1)
            s_arrived(j).wait_recv()

            compute(j)
            p_copy(j).start()

        return carry

    lax.fori_loop(0, slots + 2, work, 0)

    def settle(j, carry):
        def sent(d, carry):
            to = lax.rem(place + d, inner)
            v_copy(j, to, place).wait_send()
            c_copy(j, to, place).wait_send()
            return carry

        lax.fori_loop(1, inner, sent, 0)
        s_copy(j).wait_send()
        p_copy(j).wait_send()

        @pl.when((line < outer - 1) & (j // local <= line))
        def _():
            w_copy(j, line + 1, w_up).wait_send()

        @pl.when((line > 0) & (j // local >= line))
        def _():
            w_copy(j, line - 1, w_down).wait_send()

        return carry

    lax.fori_loop(0, slots, settle, 0)

    def got(j, carry):
        def each(d, carry):
            other = lax.rem(place + d, inner)
            r_copy(j, other, other).wait_recv()
            r_copy(j, other, place).wait_send()
            return carry

        return lax.fori_loop(1, inner, each, carry)

    lax.fori_loop(0, slots, got, 0)

    flat = ret.reshape(inner * slots * cap_pad, 128)

    def place_rows(b, carry):
        for i in range(8):
            row = b * 8 + i
            out_ref[pl.ds(row, 1), :] = flat[pl.ds(target[row], 1), :]
        return carry

    lax.fori_loop(0, out_ref.shape[0] // 8, place_rows, 0)


def visit_order(outer, local):
    steps = []
    for z in range(outer):
        order = [z * local + l for l in range(local)]
        for t in range(1, outer):
            for l in range(local):
                order += [y * local + l for y in (z - t, z + t) if 0 <= y < outer]
        steps.append(order)
    return steps


def body(peer_count, q_of_pair, q_slot, valence, conduction, screened):
    pair_count, bands, half = valence.shape
    local, g_rows, g_cols = screened.shape
    q_total = q_slot.shape[0]
    cap = max(2, (3 * pair_count + 2 * q_total - 1) // (2 * q_total))
    cap_pad = -(-cap // 8) * 8
    outer = 4 if peer_count % 4 == 0 else 1
    inner = peer_count // outer
    slots = outer * local
    rows = cap * bands
    width = -(-rows // 128) * 128

    q_ids = q_of_pair[:, 0]
    q_match = q_ids[:, None] == jnp.arange(q_total, dtype=jnp.int32)[None, :]
    slot_index = jnp.sum(jnp.where(q_match, q_slot[None, :], 0), axis=1)
    order_row = jnp.arange(pair_count, dtype=jnp.int32)
    same_q = (q_ids[:, None] == q_ids[None, :]) & (order_row[None, :] < order_row[:, None])
    rank = jnp.sum(same_q.astype(jnp.int32), axis=1)
    owner = slot_index // local
    group = owner % inner * slots + owner // inner * local + slot_index % local
    packed = group * cap + rank
    target = group * cap_pad + rank
    hit = packed[None, :] == jnp.arange(inner * slots * cap, dtype=jnp.int32)[:, None]
    source_row = jnp.sum(jnp.where(hit, order_row[None, :], 0), axis=1)

    smem = pl.BlockSpec(memory_space=pltpu.SMEM)
    anywhere = pl.BlockSpec(memory_space=pl.ANY)
    dma = pltpu.SemaphoreType.DMA
    bf16, f32 = jnp.bfloat16, jnp.float32
    return pl.pallas_call(
        functools.partial(kernel, outer, inner, local, cap, cap_pad, visit_order(outer, local)),
        out_shape=jax.ShapeDtypeStruct((pair_count, bands * bands // 2), f32),
        in_specs=[smem, smem, anywhere, anywhere, anywhere],
        out_specs=pl.BlockSpec(memory_space=pltpu.VMEM),
        scratch_shapes=[
            pltpu.VMEM((pair_count, bands, half), bf16),
            pltpu.VMEM((pair_count, bands, half), bf16),
            pltpu.VMEM((inner, slots, rows, half), bf16),
            pltpu.VMEM((inner, slots, rows, half), bf16),
            pltpu.VMEM((2, slots, inner, rows, half), bf16),
            pltpu.VMEM((slots, inner, rows, half), bf16),
            pltpu.VMEM((slots, g_rows, g_cols), bf16),
            pltpu.VMEM((inner, width, g_rows), bf16),
            pltpu.VMEM((2, slots, inner, cap_pad, 128), f32),
            pltpu.VMEM((slots, inner, cap_pad, 128), f32),
            pltpu.VMEM((inner, slots, cap_pad, 128), f32),
            pltpu.VMEM((inner, slots, cap_pad, 128), f32),
            dma((3,)), dma((slots,)), dma((slots,)), dma((slots,)),
            dma((inner * slots,)), dma((inner * slots,)),
            dma((inner * slots,)), dma((inner * slots,)),
            dma((slots,)), dma((slots,)), dma((slots,)), dma((slots,)),
            dma((inner * slots,)), dma((inner * slots,)),
        ],
        compiler_params=pltpu.CompilerParams(
            collective_id=0, has_side_effects=True, vmem_limit_bytes=58 * 1024 * 1024),
        cost_estimate=pl.CostEstimate(
            flops=2 * inner * slots * rows * g_rows * g_cols, transcendentals=0,
            bytes_accessed=4 * pair_count * bands * half + 2 * local * g_rows * g_cols),
    )(source_row, target, valence, conduction, screened)


def solution(mesh):
    in_specs = (P("pb", None), P(), P("pb", None, "ga"), P("pb", None, "ga"), P("pb", "ga", None))
    return jax.shard_map(functools.partial(body, mesh.shape["pb"]), mesh=mesh, in_specs=in_specs,
                         out_specs=P("pb", "ga"), check_vma=False)
```
